256 devices in a mesh: plane: 8 (over x, z_hi), tile: 32 (over y, z_lo, core).
Axes of the slice: x: 4, y: 4, z: 8 (z_hi: 2, z_lo: 4; z = z_hi * 4 + z_lo), core: 2. Of those that a mesh axis runs over, the one named last changes fastest.
Arguments:
- slab_cells: bfloat16 [8, 4, 4096, 4096], P('plane', None, 'tile'), may hold values from -6 to 6
- slab_weight: float32 [8, 4], P('plane'), may hold values from 0.2 to 0.6
- kernel_table: float32 [32], replicated, may hold values from 0.15 to 0.6
- kernel_index: int32 [4, 8], replicated, may hold values from 0 to 31
- ell_index: int32 [1024, 512], P('plane', 'tile'), may hold values from 0 to 16, as said below
- target_spectra: float32 [10, 16], replicated, may hold values from -1.8 to 1.8
Outputs:
- spectra: float32 [10, 16], replicated
- plane_grad: float32 [8, 4096, 4096], P('plane', 'tile')
The draws below stay inside these ranges and needn't reach their ends.
Inputs may be any that keep to these rules, and one draw needn't show every extreme that they name: `ell_index`: 16 marks a Fourier mode that enters no spectrum.
All inputs are finite; a program needn't handle non-finite values.
Results may differ from the reference program's by a relative error of at most 0.019.
Values may be sent and summed in bfloat16 or wider, within the bound.
No kernel may reach another device: no remote copies, remote signals or barrier semaphores. Data moves between devices by JAX's collectives and lax.ppermute only.
A program may use at most 128 MiB of HBM per device.

```python
import math
import jax
import jax.numpy as jnp
import numpy as np
from jax import lax

NPIX = 4096
KMAX = 512
SLAB = 4
PL_DEV = 1
BINS = 4
ELLS = 16
TABLE = 32
PLANES = 8
PAIRS = 10
N_PLANE = 8


def draw_ell_index(key, part):
    key = jax.random.fold_in(key, 7)
    wave_rows = jnp.arange(2 * KMAX, dtype=jnp.int32) - KMAX
    wave_cols = jnp.arange(KMAX, dtype=jnp.int32)
    radius_sq = wave_rows[:, None] * wave_rows[:, None] + wave_cols[None, :] * wave_cols[None, :]
    cycle_edges = jnp.arange(1, ELLS, dtype=jnp.int32) * (KMAX // ELLS)
    edge_sq = cycle_edges * cycle_edges
    radial = jnp.sum((radius_sq[:, :, None] >= edge_sq[None, None, :]).astype(jnp.int32), axis=-1)
    jitter = jax.random.randint(key, radius_sq.shape, -1, 2, dtype=jnp.int32)
    inside = jnp.clip(radial + jitter, 0, ELLS - 1)
    return jnp.where(radius_sq >= KMAX * KMAX, ELLS, inside).astype(jnp.int32)


def plant(drawn, stream_key, low, largest):
    longest = drawn.shape.index(max(drawn.shape))
    spots = []
    for shift in (0, 1):
        where = [jax.random.randint(jax.random.fold_in(stream_key, axis), (), 0, length) for axis, length in enumerate(drawn.shape)]
        where[longest] = (where[longest] + shift) % drawn.shape[longest]
        spots.append(tuple(where))
    return drawn.at[spots[0]].set(low).at[spots[1]].set(largest)


def level_of(stream_key, extent, cuts, least, high):
    def one(dim, blocks):
        heights = jax.random.uniform(jax.random.fold_in(jax.random.fold_in(stream_key, 6), dim), (blocks,), jnp.float32, least / len(cuts), high / len(cuts))
        return jnp.repeat(jnp.exp(heights), extent[dim] // blocks).reshape((-1,) + (1,) * (len(extent) - dim - 1))

    loudness = one(*cuts[0])
    for cut in cuts[1:]:
        loudness = loudness * one(*cut)
    return loudness


def normal_values(rng, extent, scale, most, cuts=(), kind=jnp.bfloat16):
    drawn = jax.random.normal(rng, extent, jnp.float32) * scale
    if len(cuts) > 0:
        drawn = level_of(rng, extent, cuts, -0.22, 0.18) * drawn
    return jnp.clip(drawn, min=-most, max=most).astype(kind)


def setup_inputs(seed: int = 0) -> dict:
    key_of = jax.random.split(jax.random.key(seed), 7)
    slab_cells = normal_values(key_of[0], (PLANES, SLAB, NPIX, NPIX), 1.0, 6.0, ((0, 8), (2, 32)))
    slab_weight = jnp.clip(jnp.exp(math.log(0.6) - 1.0986123 * jax.random.uniform(key_of[1], (PLANES, SLAB), jnp.float32) ** level_of(key_of[1], (PLANES, SLAB), ((0, 8),), -0.2, 0.2)), 0.2, 0.6)
    kernel_table = jnp.clip(jnp.exp(jax.random.uniform(key_of[2], (TABLE,), jnp.float32, math.log(0.15), math.log(0.6))), 0.15, 0.6)
    kernel_index = plant(jax.random.randint(key_of[3], (BINS, PLANES), 0, TABLE), jax.random.fold_in(key_of[3], 1), 0, TABLE - 1).astype(jnp.int32)
    ell_index = draw_ell_index(jax.random.fold_in(key_of[6], 71), 0)
    target_spectra = normal_values(key_of[5], (PAIRS, ELLS), 0.3, 1.8, (), jnp.float32)
    return {"slab_cells": slab_cells, "slab_weight": slab_weight, "kernel_table": kernel_table, "kernel_index": kernel_index, "ell_index": ell_index, "target_spectra": target_spectra}


HIGHEST = lax.Precision.HIGHEST
TWO_PI = 2.0 * math.pi

def kernel_weights(kernel_table, kernel_index):
    entries = jnp.arange(kernel_table.shape[0], dtype=jnp.int32)
    one_hot = (kernel_index[:, :, None] == entries).astype(jnp.float32)
    return jnp.einsum('bpt,t->bp', one_hot, kernel_table, precision=HIGHEST)

def column_table(start_row, amount):
    wave_num = start_row + jnp.arange(amount, dtype=jnp.int32)
    offsets = jnp.arange(NPIX, dtype=jnp.int32)
    angles = (wave_num[:, None] * offsets[None, :] % NPIX).astype(jnp.float32) * (TWO_PI / NPIX)
    stacked = jnp.stack([jnp.cos(angles), -jnp.sin(angles)], axis=1)
    return stacked.astype(jnp.bfloat16).reshape(2 * amount, NPIX)

def row_tables(start_row, amount):
    wave_num = start_row + jnp.arange(amount, dtype=jnp.int32) - KMAX
    offsets = jnp.arange(NPIX, dtype=jnp.int32)
    angles = (wave_num[:, None] * offsets[None, :] % NPIX).astype(jnp.float32) * (TWO_PI / NPIX)
    return jnp.stack([jnp.cos(angles), jnp.sin(angles)], axis=0)

def project_band(slab_rows, depth_weight, fourier_table):
    plane_map = jnp.zeros((slab_rows.shape[0], slab_rows.shape[2], slab_rows.shape[3]), jnp.float32)
    for layer_id in range(slab_rows.shape[1]):
        plane_map = plane_map + slab_rows[:, layer_id].astype(jnp.float32) * depth_weight[:, layer_id, None, None]
    plane_map = plane_map.astype(jnp.bfloat16)
    flat_rows = plane_map.reshape(-1, plane_map.shape[-1])
    band_part = lax.dot_general(fourier_table, flat_rows, (((1,), (1,)), ((), ())), preferred_element_type=jnp.float32)
    return band_part.reshape(fourier_table.shape[0] // 2, 2, plane_map.shape[0], plane_map.shape[1])

def forward_rows(tables, band_part, group_kernel):
    products = jnp.einsum('cqr,xspr->cqsxp', tables, band_part, precision=HIGHEST)
    real_part = products[0, :, 0] + products[1, :, 1]
    imag_part = products[0, :, 1] - products[1, :, 0]
    lines = jnp.stack([real_part, imag_part], axis=1)
    return jnp.einsum('qsxp,bp->qsbx', lines, group_kernel, precision=HIGHEST)

def adjoint_rows(mixed_grad, start_row, block_rows):
    row_total = mixed_grad.shape[0]
    block_size = min(row_total, block_rows)

    def one_block(block_id, running):
        offset = block_id * block_size
        section = lax.dynamic_slice_in_dim(mixed_grad, offset, block_size, 0)
        tables = row_tables(start_row + offset, block_size)
        products = jnp.einsum('cqr,qspx->csxpr', tables, section, precision=HIGHEST)
        real_part = products[0, 0] - products[1, 1]
        imag_part = products[1, 0] + products[0, 1]
        return running + jnp.stack([real_part, imag_part], axis=1)
    initial = jnp.zeros((mixed_grad.shape[3], 2, mixed_grad.shape[2], NPIX), jnp.float32)
    return lax.fori_loop(0, row_total // block_size, one_block, initial)

def column_adjoint(band_grad, fourier_table):
    flat_rows = band_grad.reshape(fourier_table.shape[0], -1)
    result = lax.dot_general(flat_rows, fourier_table, (((0,), (0,)), ((), ())), preferred_element_type=jnp.float32)
    return result.reshape(band_grad.shape[2], band_grad.shape[3], fourier_table.shape[1])

def pair_select():
    first_bin, second_bin = np.triu_indices(BINS)
    eye_bins = np.eye(BINS, dtype=np.float32)
    return (jnp.asarray(eye_bins[first_bin]), jnp.asarray(eye_bins[second_bin]))

def cycle_area():
    cycle_ids = jnp.arange(ELLS, dtype=jnp.float32)
    return (2.0 * cycle_ids + 1.0) * float((KMAX // ELLS) ** 2) * (0.5 * math.pi)

def mode_one_hot(ell_index):
    return (ell_index[:, :, None] == jnp.arange(ELLS, dtype=jnp.int32)).astype(jnp.float32)

def partial_spectra(kappa_hat, ell_index):
    pick_first, pick_second = pair_select()
    left_terms = jnp.einsum('qsbx,pb->pqsx', kappa_hat, pick_first, precision=HIGHEST)
    right_terms = jnp.einsum('qsbx,pb->pqsx', kappa_hat, pick_second, precision=HIGHEST)
    products = lax.optimization_barrier(jnp.sum(left_terms * right_terms, axis=2))
    return jnp.einsum('pqx,qxl->pl', products, mode_one_hot(ell_index), precision=HIGHEST)

def mode_gradient(kappa_hat, ell_index, spectra, target_spectra):
    pick_first, pick_second = pair_select()
    pair_mix = pick_first[:, :, None] * pick_second[:, None, :] + pick_second[:, :, None] * pick_first[:, None, :]
    weights = (spectra - target_spectra) * (KMAX / (ELLS * NPIX)) / cycle_area()
    coupling = jnp.einsum('pij,pl->lij', pair_mix, weights, precision=HIGHEST)
    per_mode = jnp.einsum('qxl,lij->qxij', mode_one_hot(ell_index), coupling, precision=HIGHEST)
    return jnp.einsum('qxij,qsjx->qsix', per_mode, kappa_hat, precision=HIGHEST)

def reference(slab_cells, slab_weight, kernel_table, kernel_index, ell_index, target_spectra):
    kernel_all = kernel_weights(kernel_table, kernel_index)
    fourier_table = column_table(0, KMAX)
    tables = row_tables(0, 2 * KMAX)
    slab_groups = slab_cells.reshape((N_PLANE, PL_DEV) + slab_cells.shape[1:])
    weight_groups = slab_weight.reshape(N_PLANE, PL_DEV, SLAB)
    kernel_groups = kernel_all.reshape(BINS, N_PLANE, PL_DEV).transpose(1, 0, 2)

    def group_term(inputs):
        slab_rows, depth_weight, group_kernel = inputs
        band_part = project_band(slab_rows, depth_weight, fourier_table)
        return forward_rows(tables, band_part, group_kernel).astype(jnp.bfloat16)
    group_terms = lax.map(group_term, (slab_groups, weight_groups, kernel_groups))
    kappa_hat = lax.optimization_barrier(jnp.sum(group_terms.astype(jnp.float32), axis=0))
    spectra = partial_spectra(kappa_hat, ell_index) / (NPIX * NPIX * cycle_area())
    grad_hat = mode_gradient(kappa_hat, ell_index, spectra, target_spectra).astype(jnp.bfloat16)

    def group_grad(group_kernel):
        mixed_grad = jnp.einsum('qsbx,bp->qspx', grad_hat.astype(jnp.float32), group_kernel, precision=HIGHEST)
        band_grad = adjoint_rows(mixed_grad, 0, 2 * KMAX)
        return column_adjoint(band_grad.astype(jnp.bfloat16), fourier_table)
    plane_grad = lax.map(group_grad, kernel_groups).reshape(PLANES, NPIX, NPIX)
    return (spectra, plane_grad)
```

```python
import functools
import math

import jax
import jax.numpy as jnp
import ml_dtypes
import numpy as np
from jax import lax
from jax.experimental import pallas as pl
from jax.experimental.pallas import tpu as pltpu
from jax.sharding import PartitionSpec as P

NPIX = 4096
KMAX = 512
BINS = 4
ELLS = 16
RADIX = 8
SPAN = NPIX // RADIX
N_PLANE = 8
N_TILE = 32
N_DEV = N_PLANE * N_TILE
ROWS = NPIX // N_TILE
LANES = 128
CHUNK = 32

ORDER = (0, 4, 1, 7, 2, 6, 3, 5)
PLACE = {rho: place for place, rho in enumerate(ORDER)}
DUOS = ((1, 7), (2, 6), (3, 5))
HALF = math.sqrt(0.5)

PAIR_ID = {}
for _number, (_i, _j) in enumerate(zip(*np.triu_indices(BINS))):
    PAIR_ID[(int(_i), int(_j))] = PAIR_ID[(int(_j), int(_i))] = _number
FIRST_GROUP = ((0, 0), (1, 1), (2, 2), (3, 3), (0, 1), (1, 2), (2, 3), (3, 0))
SECOND_GROUP = ((0, 2), (1, 3))

F32 = jnp.float32
BF16 = jnp.bfloat16
VMEM = pl.BlockSpec(memory_space=pltpu.VMEM)
SMEM = pl.BlockSpec(memory_space=pltpu.SMEM)
LIMIT = 32 * 1024 * 1024


def wave_table():
    rows = []
    tiles = np.arange(N_TILE)
    for rho in ORDER:
        k = np.concatenate([16 * tiles + 8 * kk + rho for kk in range(2)])
        m = (k[:, None] * np.arange(SPAN)[None, :]) % NPIX
        angle = 2.0 * np.pi * m / NPIX
        rows += [np.cos(angle), -np.sin(angle)]
    return np.concatenate(rows).astype(ml_dtypes.bfloat16)


def order_matrix():
    out = np.zeros((2 * KMAX, 2 * KMAX), np.float32)
    for place, rho in enumerate(ORDER):
        for sign in range(2):
            for kk in range(2):
                for t in range(N_TILE):
                    j = 16 * t + 8 * kk + rho
                    q = KMAX + j if sign == 0 else (KMAX - j if j else 0)
                    out[q, place * LANES + sign * 64 + kk * N_TILE + t] = 1.0
    return out.astype(ml_dtypes.bfloat16)


def edge_waves():
    step = lax.broadcasted_iota(jnp.int32, (1, SPAN), 1) & 7
    diag = jnp.where(step & 1 == 1, HALF, 1.0)
    cos = jnp.where(step & 3 == 2, 0.0, jnp.where((step >= 3) & (step <= 5), -diag, diag))
    sin = jnp.where(step & 3 == 0, 0.0, jnp.where(step >= 5, -diag, diag))
    return cos.astype(F32), sin.astype(F32)


def dft4(x, sign):
    (r0, i0), (r1, i1), (r2, i2), (r3, i3) = x
    ar, ai, br, bi = r0 + r2, i0 + i2, r0 - r2, i0 - i2
    cr, ci, dr, di = r1 + r3, i1 + i3, r1 - r3, i1 - i3
    if sign < 0:
        dr, di = -dr, -di
    return [(ar + cr, ai + ci), (br - di, bi + dr), (ar - cr, ai - ci), (br + di, bi - dr)]


def dft8(x, sign):
    even = dft4(x[0::2], sign)
    odd = dft4(x[1::2], sign)
    (r1, i1), (r2, i2), (r3, i3) = odd[1:]
    if sign > 0:
        turned = [odd[0], (HALF * (r1 - i1), HALF * (r1 + i1)), (-i2, r2), (-HALF * (r3 + i3), HALF * (r3 - i3))]
    else:
        turned = [odd[0], (HALF * (r1 + i1), HALF * (i1 - r1)), (i2, -r2), (HALF * (i3 - r3), -HALF * (r3 + i3))]
    low = [(a + c, b + d) for (a, b), (c, d) in zip(even, turned)]
    high = [(a - c, b - d) for (a, b), (c, d) in zip(even, turned)]
    return low + high


def dot_nt(a, b):
    return lax.dot_general(a, b, (((1,), (1,)), ((), ())), preferred_element_type=F32)


def dot_nn(a, b):
    return lax.dot_general(a, b, (((1,), (0,)), ((), ())), preferred_element_type=F32)


def dot_tn(a, b):
    return lax.dot_general(a, b, (((0,), (0,)), ((), ())), preferred_element_type=F32)


def table_of(table_ref, *rhos):
    start = PLACE[rhos[0]] * LANES
    return table_ref[start : start + LANES * len(rhos), :]


def columns_kernel(weight_ref, slab_ref, table_ref, out_ref, fold_ref, band_ref):
    step = pl.program_id(0)

    def segment(m):
        cols = slice(m * SPAN, (m + 1) * SPAN)
        total = slab_ref[0, 0, :, cols].astype(F32) * weight_ref[0, 0]
        for layer in range(1, slab_ref.shape[1]):
            total = total + slab_ref[0, layer, :, cols].astype(F32) * weight_ref[0, layer]
        return total

    def keep(index, value):
        fold_ref[index, pl.ds(pl.multiple_of(step * CHUNK, CHUNK), CHUNK), :] = value.astype(BF16)

    x0, x4 = segment(0), segment(4)
    a0, a1 = x0 + x4, x0 - x4
    x2, x6 = segment(2), segment(6)
    a2, a3 = x2 + x6, x2 - x6
    x1, x5 = segment(1), segment(5)
    b0, b1 = x1 + x5, x1 - x5
    x3, x7 = segment(3), segment(7)
    b2, b3 = x3 + x7, x3 - x7
    total, other = a0 + a2, b0 + b2
    keep(0, total + other)
    keep(1, total - other)
    minus, plus = HALF * (b1 - b3), HALF * (b1 + b3)
    keep(2, a1 + minus)
    keep(3, -a3 - plus)
    keep(4, a0 - a2)
    keep(5, b2 - b0)
    keep(6, a1 - minus)
    keep(7, a3 - plus)

    @pl.when(step == pl.num_programs(0) - 1)
    def _():
        def place(rho, re, im):
            for s, part in enumerate((re, im)):
                for kk in range(2):
                    start = rho * LANES + 2 * s + kk
                    band_ref[pl.ds(start, N_TILE, stride=4), :] = part[kk * N_TILE : (kk + 1) * N_TILE]

        for rho in (0, 4):
            got = dot_nt(table_of(table_ref, rho), fold_ref[PLACE[rho]])
            place(rho, got[:64], got[64:])
        for number, (rho, back) in enumerate(DUOS):
            pair = fold_ref[2 + 2 * number : 4 + 2 * number].reshape(2 * ROWS, SPAN)
            got = dot_nt(table_of(table_ref, rho, back), pair)
            cu, cv = got[:64, :ROWS], got[:64, ROWS:]
            su, sv = got[64:128, :ROWS], got[64:128, ROWS:]
            place(rho, cu - sv, cv + su)
            cu, cv = got[128:192, :ROWS], got[128:192, ROWS:]
            su, sv = got[192:, :ROWS], got[192:, ROWS:]
            place(back, cu + sv, su - cv)
        out_ref[...] = band_ref[...].astype(BF16)


def columns(slab, weight, table):
    return pl.pallas_call(
        columns_kernel,
        grid=(ROWS // CHUNK,),
        in_specs=[
            SMEM,
            pl.BlockSpec((1, slab.shape[1], CHUNK, NPIX), lambda i: (0, 0, i, 0)),
            pl.BlockSpec((2 * KMAX, SPAN), lambda i: (0, 0)),
        ],
        out_specs=pl.BlockSpec((2 * KMAX, ROWS), lambda i: (0, 0)),
        out_shape=jax.ShapeDtypeStruct((2 * KMAX, ROWS), BF16),
        scratch_shapes=[pltpu.VMEM((RADIX, ROWS, SPAN), BF16), pltpu.VMEM((2 * KMAX, ROWS), F32)],
        compiler_params=pltpu.CompilerParams(vmem_limit_bytes=LIMIT),
        name="columns",
    )(weight, slab, table)


def bins_kernel(plane_ref, ell_ref, order_ref, out_ref, rows_ref):
    rows_ref[...] = dot_tn(ell_ref[...], order_ref[...])
    plane = plane_ref[0]
    for kk in range(2):
        row = rows_ref[pl.ds(plane + 8 * kk, 1), :]
        out_ref[8 * kk : 8 * kk + 8, :] = jnp.broadcast_to(row, (8, 2 * KMAX)).astype(jnp.int32)


def mode_bins(plane, ell, order):
    return pl.pallas_call(
        bins_kernel,
        in_specs=[SMEM, VMEM, VMEM],
        out_specs=VMEM,
        out_shape=jax.ShapeDtypeStruct((16, 2 * KMAX), jnp.int32),
        scratch_shapes=[pltpu.VMEM((16, 2 * KMAX), F32)],
        compiler_params=pltpu.CompilerParams(vmem_limit_bytes=LIMIT),
        name="mode_bins",
    )(plane, ell, order)


def kernel_value(index_ref, values_ref, b, p):
    return values_ref[index_ref[b, p]]


def modes_kernel(index_ref, values_ref, band_ref, table_ref, ell_ref, kappa_ref, sums_ref, wide_ref, line_ref):
    wide_ref[...] = band_ref[...].astype(F32)

    def gather(m, s):
        parts = []
        for kk in range(2):
            tiles = [wide_ref[pl.ds((4 * m + u) * 4 + 2 * s + kk, N_PLANE, stride=LANES), :] for u in range(4)]
            parts.append(jnp.concatenate(tiles, axis=1))
        return jnp.concatenate(parts, axis=0)

    folded = dft8([(gather(m, 0), gather(m, 1)) for m in range(RADIX)], -1)
    low = lax.broadcasted_iota(jnp.int32, (16, LANES), 1) < 64

    def lines(rho, ahead, back):
        (cu, cv), (du, dv) = ahead, back
        real = jnp.where(low, cu - pltpu.roll(cv, 64, 1), pltpu.roll(du, 64, 1) + dv)
        imag = jnp.where(low, cv + pltpu.roll(cu, 64, 1), pltpu.roll(dv, 64, 1) - du)
        return real, imag

    def keep(rho, real, imag):
        cols = slice(PLACE[rho] * LANES, (PLACE[rho] + 1) * LANES)
        line_ref[0:16, cols] = real
        line_ref[16:32, cols] = imag

    for rho in (0, 4):
        pair = jnp.concatenate(folded[rho], axis=0).astype(BF16)
        got = dot_nt(pair, table_of(table_ref, rho))
        both = (got[:16], got[16:])
        real, imag = lines(rho, both, both)
        if rho == 0:
            cos, sin = edge_waves()
            up, vp = folded[0]
            edge_re = jnp.sum(up * cos - vp * sin, axis=1, keepdims=True)
            edge_im = jnp.sum(vp * cos + up * sin, axis=1, keepdims=True)
            edge = lax.broadcasted_iota(jnp.int32, (16, LANES), 1) == 64
            real = jnp.where(edge, edge_re, real)
            imag = jnp.where(edge, edge_im, imag)
        keep(rho, real, imag)
    for rho, back in DUOS:
        four = jnp.concatenate(folded[rho] + folded[back], axis=0).astype(BF16)
        got = dot_nt(four, table_of(table_ref, rho, back))
        for place, one in enumerate((rho, back)):
            part = got[:, place * LANES : (place + 1) * LANES]
            duo = ((part[0:16], part[16:32]), (part[32:48], part[48:64]))
            keep(one, *lines(one, duo[place], duo[1 - place]))

    bin_row = lax.broadcasted_iota(jnp.int32, (8, 1), 0) & 3
    columns_of = []
    for p in range(N_PLANE):
        column = jnp.full((8, 1), kernel_value(index_ref, values_ref, 0, p), F32)
        for b in range(1, BINS):
            column = jnp.where(bin_row == b, kernel_value(index_ref, values_ref, b, p), column)
        columns_of.append(column)
    upper = lax.broadcasted_iota(jnp.int32, (8, 2 * KMAX), 0) < 4
    first = [0.0, 0.0]
    second = [0.0, 0.0]
    for s in range(2):
        for kk in range(2):
            start = 16 * s + 8 * kk
            kappa = columns_of[0] * line_ref[start : start + 1, :]
            for p in range(1, N_PLANE):
                kappa = kappa + columns_of[p] * line_ref[start + p : start + p + 1, :]
            kappa_ref[start : start + 8, :] = kappa
            first[kk] = first[kk] + kappa * jnp.where(upper, kappa, pltpu.roll(kappa, 7, 0))
            second[kk] = second[kk] + kappa * pltpu.roll(kappa, 2, 0)

    lane = lax.broadcasted_iota(jnp.int32, (8, LANES), 1)
    spread = [jnp.zeros((8, LANES), F32), jnp.zeros((8, LANES), F32)]
    here = [ell_ref[0:8, :], ell_ref[8:16, :]]
    for ell in range(ELLS):
        for group, terms in enumerate((first, second)):
            chosen = jnp.where(here[0] == ell, terms[0], 0.0) + jnp.where(here[1] == ell, terms[1], 0.0)
            spread[group] = jnp.where(lane & 15 == ell, jnp.sum(chosen, axis=1, keepdims=True), spread[group])
    own = (lane >> 4) == lax.broadcasted_iota(jnp.int32, (8, LANES), 0)
    rows = [jnp.sum(jnp.where(own, part, 0.0), axis=0, keepdims=True) for part in spread]
    even = lax.broadcasted_iota(jnp.int32, (8, LANES), 0) & 1 == 0
    pattern = jnp.where(even, rows[0], rows[1])
    sums_ref[...] = jnp.broadcast_to(pattern[None], (N_DEV // 4, 8, LANES)).reshape(2 * N_DEV, LANES)


def modes(index, values, band, table, ell):
    return pl.pallas_call(
        modes_kernel,
        in_specs=[SMEM, SMEM, VMEM, VMEM, VMEM],
        out_specs=[VMEM, VMEM],
        out_shape=[
            jax.ShapeDtypeStruct((32, 2 * KMAX), F32),
            jax.ShapeDtypeStruct((2 * N_DEV, LANES), F32),
        ],
        scratch_shapes=[pltpu.VMEM((2 * KMAX, ROWS), F32), pltpu.VMEM((32, 2 * KMAX), F32)],
        compiler_params=pltpu.CompilerParams(vmem_limit_bytes=LIMIT),
        name="modes",
    )(index, values, band, table, ell)


def adjoint_kernel(
    index_ref, values_ref, sums_ref, kappa_ref, ell_ref, target_ref, table_ref,
    spectra_ref, out_ref, weight_ref, line_ref, wide_ref,
):
    total = jnp.sum(sums_ref[...].reshape(N_DEV // 4, 8, LANES), axis=0)
    total = total + pltpu.roll(total, 2, 0)
    total = total + pltpu.roll(total, 4, 0)
    lane = lax.broadcasted_iota(jnp.int32, (1, LANES), 1)
    area = (2.0 * lane.astype(F32) + 1.0) * (float((KMAX // ELLS) ** 2) * (0.5 * math.pi))
    scale = float(NPIX * NPIX) * area
    for row, group in enumerate((FIRST_GROUP, SECOND_GROUP)):
        line = total[row : row + 1, :]
        for place, pair in enumerate(group):
            turned = line if place == 0 else pltpu.roll(line, LANES - 16 * place, 1)
            number = PAIR_ID[pair]
            spectra_ref[number : number + 1, :] = (turned / scale)[:, :ELLS]
    weight_ref[...] = jnp.zeros_like(weight_ref)
    weight_ref[0:10, 0:ELLS] = (spectra_ref[...] - target_ref[...]) * (
        float(KMAX) / (ELLS * NPIX)
    ) / area[:, :ELLS]

    bin_row = lax.broadcasted_iota(jnp.int32, (8, LANES), 0) & 3
    couplings = []
    for j in range(BINS):
        mixed = None
        for i in range(BINS):
            number = PAIR_ID[(i, j)]
            row = weight_ref[number : number + 1, :]
            row = row + row if i == j else row
            mixed = jnp.broadcast_to(row, (8, LANES)) if mixed is None else jnp.where(bin_row == i, row, mixed)
        couplings.append(mixed)
    plane_row = lax.broadcasted_iota(jnp.int32, (8, 1), 0)
    columns_of = []
    for b in range(BINS):
        column = jnp.full((8, 1), kernel_value(index_ref, values_ref, b, 0), F32)
        for p in range(1, N_PLANE):
            column = jnp.where(plane_row == p, kernel_value(index_ref, values_ref, b, p), column)
        columns_of.append(column)

    for tile in range(RADIX):
        cols = slice(tile * LANES, (tile + 1) * LANES)
        for kk in range(2):
            where = ell_ref[8 * kk : 8 * kk + 8, cols]
            mixers = [jnp.take_along_axis(table, where, axis=1) for table in couplings]
            for s in range(2):
                start = 16 * s + 8 * kk
                grad = mixers[0] * kappa_ref[start : start + 1, cols]
                for j in range(1, BINS):
                    grad = grad + mixers[j] * kappa_ref[start + j : start + j + 1, cols]
                grad = grad.astype(BF16).astype(F32)
                line = columns_of[0] * grad[0:1]
                for b in range(1, BINS):
                    line = line + columns_of[b] * grad[b : b + 1]
                line_ref[start : start + 8, cols] = line

    wide_lane = lax.broadcasted_iota(jnp.int32, (16, LANES), 1)
    low = wide_lane < 64

    def factors(rho):
        cols = slice(PLACE[rho] * LANES, (PLACE[rho] + 1) * LANES)
        g0, g1 = line_ref[0:16, cols], line_ref[16:32, cols]
        if rho == 0:
            g0 = jnp.where(wide_lane == 64, 0.0, g0)
            g1 = jnp.where(wide_lane == 64, 0.0, g1)
        t0, t1 = pltpu.roll(g0, 64, 1), pltpu.roll(g1, 64, 1)
        ahead = (jnp.where(low, g0, t1), jnp.where(low, g1, -t0))
        back = (jnp.where(low, t0, -g1), jnp.where(low, t1, g0))
        return ahead, back

    spread = [None] * RADIX
    for rho in (0, 4):
        ahead, back = factors(rho)
        left = jnp.concatenate([ahead[0] + back[0], ahead[1] + back[1]], axis=0).astype(BF16)
        got = dot_nn(left, table_of(table_ref, rho))
        spread[rho] = (got[:16], got[16:])
    start = PLACE[0] * LANES + 64
    edge0 = line_ref[0:16, start : start + 1]
    edge1 = line_ref[16:32, start : start + 1]
    cos, sin = edge_waves()
    spread[0] = (spread[0][0] + edge0 * cos + edge1 * sin, spread[0][1] + edge1 * cos - edge0 * sin)
    for rho, back in DUOS:
        plus, minus = factors(rho)
        plus_back, minus_back = factors(back)
        left = jnp.concatenate(
            [
                jnp.concatenate(plus + minus, axis=0),
                jnp.concatenate(minus_back + plus_back, axis=0),
            ],
            axis=1,
        ).astype(BF16)
        got = dot_nn(left, table_of(table_ref, rho, back))
        spread[rho] = (got[0:16], got[16:32])
        spread[back] = (got[32:48], got[48:64])
    for m, both in enumerate(dft8(spread, 1)):
        for s in range(2):
            for kk in range(2):
                for u in range(4):
                    begin = (4 * m + u) * 4 + 2 * s + kk
                    wide_ref[pl.ds(begin, N_PLANE, stride=LANES), :] = both[s][
                        8 * kk : 8 * kk + 8, u * LANES : (u + 1) * LANES
                    ]
    out_ref[...] = wide_ref[...].astype(BF16)


def adjoint(index, values, sums, kappa, ell, target, table):
    return pl.pallas_call(
        adjoint_kernel,
        in_specs=[SMEM, SMEM, VMEM, VMEM, VMEM, VMEM, VMEM],
        out_specs=[VMEM, VMEM],
        out_shape=[
            jax.ShapeDtypeStruct(target.shape, F32),
            jax.ShapeDtypeStruct((2 * KMAX, ROWS), BF16),
        ],
        scratch_shapes=[
            pltpu.VMEM((16, LANES), F32),
            pltpu.VMEM((32, 2 * KMAX), F32),
            pltpu.VMEM((2 * KMAX, ROWS), F32),
        ],
        compiler_params=pltpu.CompilerParams(vmem_limit_bytes=LIMIT),
        name="adjoint",
    )(index, values, sums, kappa, ell, target, table)


def maps_kernel(band_ref, table_ref, out_ref, wide_ref):
    wide_ref[...] = band_ref[...].astype(F32)

    def block(rho, s):
        parts = [
            wide_ref[pl.ds(rho * LANES + 2 * s + kk, N_TILE, stride=4), :] for kk in range(2)
        ]
        return jnp.concatenate(parts, axis=0)

    flat = []
    for rho in (0, 4):
        left = jnp.concatenate([block(rho, 0), block(rho, 1)], axis=0).astype(BF16)
        flat.append(dot_tn(left, table_of(table_ref, rho)))
    p, q = [None], [None]
    for rho, back in DUOS:
        b0, b1, e0, e1 = block(rho, 0), block(rho, 1), block(back, 0), block(back, 1)
        left = jnp.concatenate(
            [
                jnp.concatenate([b0, b1, e0, e1], axis=0),
                jnp.concatenate([b1, -b0, -e1, e0], axis=0),
            ],
            axis=1,
        ).astype(BF16)
        got = dot_tn(left, table_of(table_ref, rho, back))
        p.append(got[:ROWS])
        q.append(got[ROWS:])
    plus, minus = flat[0] + flat[1], flat[0] - flat[1]

    def put(m, even, odd):
        out_ref[0, :, m * SPAN : (m + 1) * SPAN] = even + odd
        out_ref[0, :, (m + 4) * SPAN : (m + 5) * SPAN] = even - odd

    put(0, plus + p[2], p[1] + p[3])
    put(1, minus - q[2], HALF * (p[1] - q[1] - p[3] - q[3]))
    put(2, plus - p[2], q[3] - q[1])
    put(3, minus + q[2], HALF * (p[3] - p[1] - q[1] - q[3]))


def maps(band, table):
    return pl.pallas_call(
        maps_kernel,
        in_specs=[VMEM, VMEM],
        out_specs=VMEM,
        out_shape=jax.ShapeDtypeStruct((1, ROWS, NPIX), F32),
        scratch_shapes=[pltpu.VMEM((2 * KMAX, ROWS), F32)],
        compiler_params=pltpu.CompilerParams(vmem_limit_bytes=LIMIT),
        name="maps",
    )(band, table)


def body(slab_cells, slab_weight, kernel_table, kernel_index, ell_index, target_spectra):
    table = jnp.asarray(wave_table())
    order = jnp.asarray(order_matrix())
    exchange = functools.partial(
        lax.all_to_all, axis_name=("plane", "tile"), split_axis=0, concat_axis=0, tiled=True
    )
    plane = lax.axis_index("plane").astype(jnp.int32).reshape(1)
    ell_rows = lax.all_gather(ell_index.astype(BF16), "plane", axis=0, tiled=True)
    band = exchange(columns(slab_cells, slab_weight, table))
    ell = mode_bins(plane, ell_rows, order)
    kappa, sums = modes(kernel_index, kernel_table, band, table, ell)
    sums = exchange(sums)
    spectra, adjoint_band = adjoint(
        kernel_index, kernel_table, sums, kappa, ell, target_spectra, table
    )
    return spectra, maps(exchange(adjoint_band), table)


def solution(mesh):
    return jax.shard_map(
        body,
        mesh=mesh,
        in_specs=(
            P("plane", None, "tile", None),
            P("plane", None),
            P(),
            P(),
            P("plane", "tile"),
            P(),
        ),
        out_specs=(P(), P("plane", "tile", None)),
        check_vma=False,
    )
```

```python
import functools
import math

import jax
import jax.numpy as jnp
import ml_dtypes
import numpy as np
from jax import lax
from jax.experimental import pallas as pl
from jax.experimental.pallas import tpu as pltpu
from jax.sharding import PartitionSpec as P

NPIX = 4096
KMAX = 512
BINS = 4
ELLS = 16
RADIX = 8
SPAN = NPIX // RADIX
N_PLANE = 8
N_TILE = 32
N_DEV = N_PLANE * N_TILE
ROWS = NPIX // N_TILE
LANES = 128
CHUNK = 16
PACK = 6
CHUNKS = ROWS // CHUNK

ORDER = (0, 4, 1, 7, 2, 6, 3, 5)
PLACE = {rho: place for place, rho in enumerate(ORDER)}
DUOS = ((1, 7), (2, 6), (3, 5))
HALF = math.sqrt(0.5)

PAIR_ID = {}
for _number, (_i, _j) in enumerate(zip(*np.triu_indices(BINS))):
    PAIR_ID[(int(_i), int(_j))] = PAIR_ID[(int(_j), int(_i))] = _number
FIRST_GROUP = ((0, 0), (1, 1), (2, 2), (3, 3), (0, 1), (1, 2), (2, 3), (3, 0))
SECOND_GROUP = ((0, 2), (1, 3))

F32 = jnp.float32
BF16 = jnp.bfloat16
VMEM = pl.BlockSpec(memory_space=pltpu.VMEM)
SMEM = pl.BlockSpec(memory_space=pltpu.SMEM)
LIMIT = 32 * 1024 * 1024


def wave_table():
    rows = []
    tiles = np.arange(N_TILE)
    for rho in ORDER:
        k = np.concatenate([16 * tiles + 8 * kk + rho for kk in range(2)])
        m = (k[:, None] * np.arange(SPAN)[None, :]) % NPIX
        angle = 2.0 * np.pi * m / NPIX
        rows += [np.cos(angle), -np.sin(angle)]
    return np.concatenate(rows).astype(ml_dtypes.bfloat16)


def order_matrix():
    out = np.zeros((2 * KMAX, 2 * KMAX), np.float32)
    for place, rho in enumerate(ORDER):
        for sign in range(2):
            for kk in range(2):
                for t in range(N_TILE):
                    j = 16 * t + 8 * kk + rho
                    q = KMAX + j if sign == 0 else (KMAX - j if j else 0)
                    out[q, place * LANES + sign * 64 + kk * N_TILE + t] = 1.0
    return out.astype(ml_dtypes.bfloat16)


def edge_waves():
    step = lax.broadcasted_iota(jnp.int32, (1, SPAN), 1) & 7
    diag = jnp.where(step & 1 == 1, HALF, 1.0)
    cos = jnp.where(step & 3 == 2, 0.0, jnp.where((step >= 3) & (step <= 5), -diag, diag))
    sin = jnp.where(step & 3 == 0, 0.0, jnp.where(step >= 5, -diag, diag))
    return cos.astype(F32), sin.astype(F32)


def dft4(x, sign):
    (r0, i0), (r1, i1), (r2, i2), (r3, i3) = x
    ar, ai, br, bi = r0 + r2, i0 + i2, r0 - r2, i0 - i2
    cr, ci, dr, di = r1 + r3, i1 + i3, r1 - r3, i1 - i3
    if sign < 0:
        dr, di = -dr, -di
    return [(ar + cr, ai + ci), (br - di, bi + dr), (ar - cr, ai - ci), (br + di, bi - dr)]


def dft8(x, sign):
    even = dft4(x[0::2], sign)
    odd = dft4(x[1::2], sign)
    (r1, i1), (r2, i2), (r3, i3) = odd[1:]
    if sign > 0:
        turned = [odd[0], (HALF * (r1 - i1), HALF * (r1 + i1)), (-i2, r2), (-HALF * (r3 + i3), HALF * (r3 - i3))]
    else:
        turned = [odd[0], (HALF * (r1 + i1), HALF * (i1 - r1)), (i2, -r2), (HALF * (i3 - r3), -HALF * (r3 + i3))]
    low = [(a + c, b + d) for (a, b), (c, d) in zip(even, turned)]
    high = [(a - c, b - d) for (a, b), (c, d) in zip(even, turned)]
    return low + high


def dot_nt(a, b):
    return lax.dot_general(a, b, (((1,), (1,)), ((), ())), preferred_element_type=F32)


def dot_nn(a, b):
    return lax.dot_general(a, b, (((1,), (0,)), ((), ())), preferred_element_type=F32)


def dot_tn(a, b):
    return lax.dot_general(a, b, (((0,), (0,)), ((), ())), preferred_element_type=F32)


def table_of(table_ref, *rhos):
    start = PLACE[rhos[0]] * LANES
    return table_ref[start : start + LANES * len(rhos), :]


def columns_kernel(
    weight_ref, slab_ref, ell_ref, table_ref, out_ref, cells_ref, held_ref, fold_ref, band_ref,
    scale_ref, bins_ref, sems, table_sem, small_sems,
):
    def fetch(chunk):
        rows = pl.ds(chunk * CHUNK, CHUNK)
        return pltpu.make_async_copy(slab_ref.at[0, :, rows, :], cells_ref.at[chunk], sems.at[chunk])

    def fetch_table():
        return pltpu.make_async_copy(table_ref, held_ref, table_sem)

    for chunk in range(CHUNKS):
        fetch(chunk).start(priority=chunk % 2)
    small = (
        pltpu.make_async_copy(weight_ref, scale_ref, small_sems.at[0]),
        pltpu.make_async_copy(ell_ref, bins_ref, small_sems.at[1]),
    )
    for copy in small:
        copy.start()
    fetch_table().start()
    for copy in small:
        copy.wait()
    weights = [scale_ref[0, layer] for layer in range(slab_ref.shape[1])]

    def butterfly(chunk, start):
        def segment(m):
            cols = slice(m * SPAN + start, m * SPAN + start + LANES)
            total = cells_ref[chunk, 0, :, cols].astype(F32) * weights[0]
            for layer in range(1, len(weights)):
                total = total + cells_ref[chunk, layer, :, cols].astype(F32) * weights[layer]
            return total

        def keep(index, value):
            fold_ref[index, chunk * CHUNK : (chunk + 1) * CHUNK, start : start + LANES] = value.astype(BF16)

        x0, x4 = segment(0), segment(4)
        a0, a1 = x0 + x4, x0 - x4
        x2, x6 = segment(2), segment(6)
        a2, a3 = x2 + x6, x2 - x6
        x1, x5 = segment(1), segment(5)
        b0, b1 = x1 + x5, x1 - x5
        x3, x7 = segment(3), segment(7)
        b2, b3 = x3 + x7, x3 - x7
        total, other = a0 + a2, b0 + b2
        keep(0, total + other)
        keep(1, total - other)
        minus, plus = HALF * (b1 - b3), HALF * (b1 + b3)
        keep(2, a1 + minus)
        keep(3, -a3 - plus)
        keep(4, a0 - a2)
        keep(5, b2 - b0)
        keep(6, a1 - minus)
        keep(7, a3 - plus)

    for p in range(N_PLANE):
        for kk in range(2):
            line = bins_ref[p + 8 * kk : p + 8 * kk + 1, :].astype(F32)
            start = p * N_TILE * PACK + 4 + kk
            band_ref[pl.ds(start, N_TILE, stride=PACK), :] = jnp.broadcast_to(line, (N_TILE, ROWS))

    for chunk in range(CHUNKS):
        fetch(chunk).wait()
        for start in range(0, SPAN, LANES):
            butterfly(chunk, start)
    fetch_table().wait()

    def place(rho, re, im):
        for s, part in enumerate((re, im)):
            for kk in range(2):
                start = rho * N_TILE * PACK + 2 * s + kk
                band_ref[pl.ds(start, N_TILE, stride=PACK), :] = part[kk * N_TILE : (kk + 1) * N_TILE]

    for rho in (0, 4):
        got = dot_nt(table_of(held_ref, rho), fold_ref[PLACE[rho]])
        place(rho, got[:64], got[64:])
    for number, (rho, back) in enumerate(DUOS):
        pair = fold_ref[2 + 2 * number : 4 + 2 * number].reshape(2 * ROWS, SPAN)
        got = dot_nt(table_of(held_ref, rho, back), pair)
        cu, cv = got[:64, :ROWS], got[:64, ROWS:]
        su, sv = got[64:128, :ROWS], got[64:128, ROWS:]
        place(rho, cu - sv, cv + su)
        cu, cv = got[128:192, :ROWS], got[128:192, ROWS:]
        su, sv = got[192:, :ROWS], got[192:, ROWS:]
        place(back, cu + sv, su - cv)
    out_ref[...] = band_ref[...].astype(BF16)


def columns(slab, weight, ell, table):
    hbm = pl.BlockSpec(memory_space=pltpu.HBM)
    return pl.pallas_call(
        columns_kernel,
        in_specs=[hbm] * 4,
        out_specs=VMEM,
        out_shape=jax.ShapeDtypeStruct((N_DEV * PACK, ROWS), BF16),
        scratch_shapes=[
            pltpu.VMEM((CHUNKS, slab.shape[1], CHUNK, NPIX), BF16),
            pltpu.VMEM(table.shape, BF16),
            pltpu.VMEM((RADIX, ROWS, SPAN), BF16),
            pltpu.VMEM((N_DEV * PACK, ROWS), F32),
            pltpu.SMEM(weight.shape, F32),
            pltpu.VMEM(ell.shape, jnp.int32),
            pltpu.SemaphoreType.DMA((CHUNKS,)),
            pltpu.SemaphoreType.DMA,
            pltpu.SemaphoreType.DMA((2,)),
        ],
        compiler_params=pltpu.CompilerParams(vmem_limit_bytes=60 * 1024 * 1024),
        name="columns",
    )(weight, slab, ell, table)


def kernel_value(index_ref, values_ref, b, p):
    return values_ref[index_ref[b, p]]


def modes_kernel(
    tile_ref, index_ref, values_ref, band_ref, table_ref, order_ref,
    kappa_ref, sums_ref, ell_ref, wide_ref, line_ref,
):
    wide_ref[...] = band_ref[...].astype(F32)
    bins = tile_ref[0] * PACK + 4
    for kk in range(2):
        parts = [wide_ref[pl.ds(bins + p * N_TILE * PACK + kk, 1), :] for p in range(N_PLANE)]
        line = jnp.broadcast_to(jnp.concatenate(parts, axis=1), (16, 2 * KMAX)).astype(BF16)
        ell_ref[8 * kk : 8 * kk + 8, :] = dot_nn(line, order_ref[...])[:8].astype(jnp.int32)

    def gather(m, s):
        parts = []
        for kk in range(2):
            tiles = [wide_ref[pl.ds((4 * m + u) * PACK + 2 * s + kk, N_PLANE, stride=N_TILE * PACK), :] for u in range(4)]
            parts.append(jnp.concatenate(tiles, axis=1))
        return jnp.concatenate(parts, axis=0)

    folded = dft8([(gather(m, 0), gather(m, 1)) for m in range(RADIX)], -1)
    low = lax.broadcasted_iota(jnp.int32, (16, LANES), 1) < 64

    def lines(rho, ahead, back):
        (cu, cv), (du, dv) = ahead, back
        real = jnp.where(low, cu - pltpu.roll(cv, 64, 1), pltpu.roll(du, 64, 1) + dv)
        imag = jnp.where(low, cv + pltpu.roll(cu, 64, 1), pltpu.roll(dv, 64, 1) - du)
        return real, imag

    def keep(rho, real, imag):
        cols = slice(PLACE[rho] * LANES, (PLACE[rho] + 1) * LANES)
        line_ref[0:16, cols] = real
        line_ref[16:32, cols] = imag

    for rho in (0, 4):
        pair = jnp.concatenate(folded[rho], axis=0).astype(BF16)
        got = dot_nt(pair, table_of(table_ref, rho))
        both = (got[:16], got[16:])
        real, imag = lines(rho, both, both)
        if rho == 0:
            cos, sin = edge_waves()
            up, vp = folded[0]
            edge_re = jnp.sum(up * cos - vp * sin, axis=1, keepdims=True)
            edge_im = jnp.sum(vp * cos + up * sin, axis=1, keepdims=True)
            edge = lax.broadcasted_iota(jnp.int32, (16, LANES), 1) == 64
            real = jnp.where(edge, edge_re, real)
            imag = jnp.where(edge, edge_im, imag)
        keep(rho, real, imag)
    for rho, back in DUOS:
        four = jnp.concatenate(folded[rho] + folded[back], axis=0).astype(BF16)
        got = dot_nt(four, table_of(table_ref, rho, back))
        for place, one in enumerate((rho, back)):
            part = got[:, place * LANES : (place + 1) * LANES]
            duo = ((part[0:16], part[16:32]), (part[32:48], part[48:64]))
            keep(one, *lines(one, duo[place], duo[1 - place]))

    bin_row = lax.broadcasted_iota(jnp.int32, (8, 1), 0) & 3
    columns_of = []
    for p in range(N_PLANE):
        column = jnp.full((8, 1), kernel_value(index_ref, values_ref, 0, p), F32)
        for b in range(1, BINS):
            column = jnp.where(bin_row == b, kernel_value(index_ref, values_ref, b, p), column)
        columns_of.append(column)
    upper = lax.broadcasted_iota(jnp.int32, (8, 2 * KMAX), 0) < 4
    first = [0.0, 0.0]
    second = [0.0, 0.0]
    for s in range(2):
        for kk in range(2):
            start = 16 * s + 8 * kk
            kappa = columns_of[0] * line_ref[start : start + 1, :]
            for p in range(1, N_PLANE):
                kappa = kappa + columns_of[p] * line_ref[start + p : start + p + 1, :]
            kappa_ref[start : start + 8, :] = kappa
            first[kk] = first[kk] + kappa * jnp.where(upper, kappa, pltpu.roll(kappa, 7, 0))
            second[kk] = second[kk] + kappa * pltpu.roll(kappa, 2, 0)

    lane = lax.broadcasted_iota(jnp.int32, (8, LANES), 1)
    spread = [jnp.zeros((8, LANES), F32), jnp.zeros((8, LANES), F32)]
    here = [ell_ref[0:8, :], ell_ref[8:16, :]]
    for ell in range(ELLS):
        for group, terms in enumerate((first, second)):
            chosen = jnp.where(here[0] == ell, terms[0], 0.0) + jnp.where(here[1] == ell, terms[1], 0.0)
            spread[group] = jnp.where(lane & 15 == ell, jnp.sum(chosen, axis=1, keepdims=True), spread[group])
    own = (lane >> 4) == lax.broadcasted_iota(jnp.int32, (8, LANES), 0)
    rows = [jnp.sum(jnp.where(own, part, 0.0), axis=0, keepdims=True) for part in spread]
    even = lax.broadcasted_iota(jnp.int32, (8, LANES), 0) & 1 == 0
    pattern = jnp.where(even, rows[0], rows[1])
    sums_ref[...] = jnp.broadcast_to(pattern[None], (N_DEV // 4, 8, LANES)).reshape(2 * N_DEV, LANES)


def modes(tile, index, values, band, table, order):
    return pl.pallas_call(
        modes_kernel,
        in_specs=[SMEM, SMEM, SMEM, VMEM, VMEM, VMEM],
        out_specs=[VMEM, VMEM, VMEM],
        out_shape=[
            jax.ShapeDtypeStruct((32, 2 * KMAX), F32),
            jax.ShapeDtypeStruct((2 * N_DEV, LANES), F32),
            jax.ShapeDtypeStruct((16, 2 * KMAX), jnp.int32),
        ],
        scratch_shapes=[pltpu.VMEM((N_DEV * PACK, ROWS), F32), pltpu.VMEM((32, 2 * KMAX), F32)],
        compiler_params=pltpu.CompilerParams(vmem_limit_bytes=LIMIT),
        name="modes",
    )(tile, index, values, band, table, order)


def adjoint_kernel(
    index_ref, values_ref, sums_ref, kappa_ref, ell_ref, target_ref, table_ref,
    spectra_ref, out_ref, weight_ref, line_ref, wide_ref,
):
    total = jnp.sum(sums_ref[...].reshape(N_DEV // 4, 8, LANES), axis=0)
    total = total + pltpu.roll(total, 2, 0)
    total = total + pltpu.roll(total, 4, 0)
    lane = lax.broadcasted_iota(jnp.int32, (1, LANES), 1)
    area = (2.0 * lane.astype(F32) + 1.0) * (float((KMAX // ELLS) ** 2) * (0.5 * math.pi))
    scale = float(NPIX * NPIX) * area
    for row, group in enumerate((FIRST_GROUP, SECOND_GROUP)):
        line = total[row : row + 1, :]
        for place, pair in enumerate(group):
            turned = line if place == 0 else pltpu.roll(line, LANES - 16 * place, 1)
            number = PAIR_ID[pair]
            spectra_ref[number : number + 1, :] = (turned / scale)[:, :ELLS]
    weight_ref[...] = jnp.zeros_like(weight_ref)
    weight_ref[0:10, 0:ELLS] = (spectra_ref[...] - target_ref[...]) * (
        float(KMAX) / (ELLS * NPIX)
    ) / area[:, :ELLS]

    bin_row = lax.broadcasted_iota(jnp.int32, (8, LANES), 0) & 3
    couplings = []
    for j in range(BINS):
        mixed = None
        for i in range(BINS):
            number = PAIR_ID[(i, j)]
            row = weight_ref[number : number + 1, :]
            row = row + row if i == j else row
            mixed = jnp.broadcast_to(row, (8, LANES)) if mixed is None else jnp.where(bin_row == i, row, mixed)
        couplings.append(mixed)
    plane_row = lax.broadcasted_iota(jnp.int32, (8, 1), 0)
    columns_of = []
    for b in range(BINS):
        column = jnp.full((8, 1), kernel_value(index_ref, values_ref, b, 0), F32)
        for p in range(1, N_PLANE):
            column = jnp.where(plane_row == p, kernel_value(index_ref, values_ref, b, p), column)
        columns_of.append(column)

    for tile in range(RADIX):
        cols = slice(tile * LANES, (tile + 1) * LANES)
        for kk in range(2):
            where = ell_ref[8 * kk : 8 * kk + 8, cols]
            mixers = [jnp.take_along_axis(table, where, axis=1) for table in couplings]
            for s in range(2):
                start = 16 * s + 8 * kk
                grad = mixers[0] * kappa_ref[start : start + 1, cols]
                for j in range(1, BINS):
                    grad = grad + mixers[j] * kappa_ref[start + j : start + j + 1, cols]
                grad = grad.astype(BF16).astype(F32)
                line = columns_of[0] * grad[0:1]
                for b in range(1, BINS):
                    line = line + columns_of[b] * grad[b : b + 1]
                line_ref[start : start + 8, cols] = line

    wide_lane = lax.broadcasted_iota(jnp.int32, (16, LANES), 1)
    low = wide_lane < 64

    def factors(rho):
        cols = slice(PLACE[rho] * LANES, (PLACE[rho] + 1) * LANES)
        g0, g1 = line_ref[0:16, cols], line_ref[16:32, cols]
        if rho == 0:
            g0 = jnp.where(wide_lane == 64, 0.0, g0)
            g1 = jnp.where(wide_lane == 64, 0.0, g1)
        t0, t1 = pltpu.roll(g0, 64, 1), pltpu.roll(g1, 64, 1)
        ahead = (jnp.where(low, g0, t1), jnp.where(low, g1, -t0))
        back = (jnp.where(low, t0, -g1), jnp.where(low, t1, g0))
        return ahead, back

    spread = [None] * RADIX
    for rho in (0, 4):
        ahead, back = factors(rho)
        left = jnp.concatenate([ahead[0] + back[0], ahead[1] + back[1]], axis=0).astype(BF16)
        got = dot_nn(left, table_of(table_ref, rho))
        spread[rho] = (got[:16], got[16:])
    start = PLACE[0] * LANES + 64
    edge0 = line_ref[0:16, start : start + 1]
    edge1 = line_ref[16:32, start : start + 1]
    cos, sin = edge_waves()
    spread[0] = (spread[0][0] + edge0 * cos + edge1 * sin, spread[0][1] + edge1 * cos - edge0 * sin)
    for rho, back in DUOS:
        plus, minus = factors(rho)
        plus_back, minus_back = factors(back)
        left = jnp.concatenate(
            [
                jnp.concatenate(plus + minus, axis=0),
                jnp.concatenate(minus_back + plus_back, axis=0),
            ],
            axis=1,
        ).astype(BF16)
        got = dot_nn(left, table_of(table_ref, rho, back))
        spread[rho] = (got[0:16], got[16:32])
        spread[back] = (got[32:48], got[48:64])
    for m, both in enumerate(dft8(spread, 1)):
        for s in range(2):
            for kk in range(2):
                for u in range(4):
                    begin = (4 * m + u) * 4 + 2 * s + kk
                    wide_ref[pl.ds(begin, N_PLANE, stride=LANES), :] = both[s][
                        8 * kk : 8 * kk + 8, u * LANES : (u + 1) * LANES
                    ]
    out_ref[...] = wide_ref[...].astype(BF16)


def adjoint(index, values, sums, kappa, ell, target, table):
    return pl.pallas_call(
        adjoint_kernel,
        in_specs=[SMEM, SMEM, VMEM, VMEM, VMEM, VMEM, VMEM],
        out_specs=[VMEM, VMEM],
        out_shape=[
            jax.ShapeDtypeStruct(target.shape, F32),
            jax.ShapeDtypeStruct((2 * KMAX, ROWS), BF16),
        ],
        scratch_shapes=[
            pltpu.VMEM((16, LANES), F32),
            pltpu.VMEM((32, 2 * KMAX), F32),
            pltpu.VMEM((2 * KMAX, ROWS), F32),
        ],
        compiler_params=pltpu.CompilerParams(vmem_limit_bytes=LIMIT),
        name="adjoint",
    )(index, values, sums, kappa, ell, target, table)


def maps_kernel(band_ref, table_ref, out_ref, wide_ref):
    wide_ref[...] = band_ref[...].astype(F32)

    def block(rho, s):
        parts = [
            wide_ref[pl.ds(rho * LANES + 2 * s + kk, N_TILE, stride=4), :] for kk in range(2)
        ]
        return jnp.concatenate(parts, axis=0)

    flat = []
    for rho in (0, 4):
        left = jnp.concatenate([block(rho, 0), block(rho, 1)], axis=0).astype(BF16)
        flat.append(dot_tn(left, table_of(table_ref, rho)))
    p, q = [None], [None]
    for rho, back in DUOS:
        b0, b1, e0, e1 = block(rho, 0), block(rho, 1), block(back, 0), block(back, 1)
        left = jnp.concatenate(
            [
                jnp.concatenate([b0, b1, e0, e1], axis=0),
                jnp.concatenate([b1, -b0, -e1, e0], axis=0),
            ],
            axis=1,
        ).astype(BF16)
        got = dot_tn(left, table_of(table_ref, rho, back))
        p.append(got[:ROWS])
        q.append(got[ROWS:])
    plus, minus = flat[0] + flat[1], flat[0] - flat[1]

    def put(m, even, odd):
        out_ref[0, :, m * SPAN : (m + 1) * SPAN] = even + odd
        out_ref[0, :, (m + 4) * SPAN : (m + 5) * SPAN] = even - odd

    put(0, plus + p[2], p[1] + p[3])
    put(1, minus - q[2], HALF * (p[1] - q[1] - p[3] - q[3]))
    put(2, plus - p[2], q[3] - q[1])
    put(3, minus + q[2], HALF * (p[3] - p[1] - q[1] - q[3]))


def maps(band, table):
    return pl.pallas_call(
        maps_kernel,
        in_specs=[VMEM, VMEM],
        out_specs=VMEM,
        out_shape=jax.ShapeDtypeStruct((1, ROWS, NPIX), F32),
        scratch_shapes=[pltpu.VMEM((2 * KMAX, ROWS), F32)],
        compiler_params=pltpu.CompilerParams(vmem_limit_bytes=LIMIT),
        name="maps",
    )(band, table)


def body(slab_cells, slab_weight, kernel_table, kernel_index, ell_index, target_spectra):
    table = jnp.asarray(wave_table())
    order = jnp.asarray(order_matrix())
    exchange = functools.partial(
        lax.all_to_all, axis_name=("plane", "tile"), split_axis=0, concat_axis=0, tiled=True
    )
    tile = lax.axis_index("tile").astype(jnp.int32).reshape(1)
    band = columns(slab_cells, slab_weight, ell_index.T, table)
    band = exchange(band.reshape(-1, 2, ROWS)).reshape(-1, ROWS)
    kappa, sums, ell = modes(tile, kernel_index, kernel_table, band, table, order)
    sums = exchange(sums)
    spectra, adjoint_band = adjoint(
        kernel_index, kernel_table, sums, kappa, ell, target_spectra, table
    )
    return spectra, maps(exchange(adjoint_band), table)


def solution(mesh):
    return jax.shard_map(
        body,
        mesh=mesh,
        in_specs=(
            P("plane", None, "tile", None),
            P("plane", None),
            P(),
            P(),
            P("plane", "tile"),
            P(),
        ),
        out_specs=(P(), P("plane", "tile", None)),
        check_vma=False,
    )
```

```python
import functools
import math

import jax
import jax.numpy as jnp
import ml_dtypes
import numpy as np
from jax import lax
from jax.experimental import pallas as pl
from jax.experimental.pallas import tpu as pltpu
from jax.sharding import PartitionSpec as P

NPIX = 4096
KMAX = 512
BINS = 4
ELLS = 16
RADIX = 8
SPAN = NPIX // RADIX
N_PLANE = 8
N_TILE = 32
ROWS = NPIX // N_TILE
LANES = 128
CHUNK = 16
WIDTH = 2 * KMAX + ROWS
PAIRS = BINS * (BINS + 1) // 2
CHUNKS = ROWS // CHUNK

ORDER = (0, 4, 1, 7, 2, 6, 3, 5)
PLACE = {rho: place for place, rho in enumerate(ORDER)}
DUOS = ((1, 7), (2, 6), (3, 5))
HALF = math.sqrt(0.5)

PAIR_ID = {}
for _number, (_i, _j) in enumerate(zip(*np.triu_indices(BINS))):
    PAIR_ID[(int(_i), int(_j))] = PAIR_ID[(int(_j), int(_i))] = _number
FIRST_GROUP = ((0, 0), (1, 1), (2, 2), (3, 3), (0, 1), (1, 2), (2, 3), (3, 0))
SECOND_GROUP = ((0, 2), (1, 3))

F32 = jnp.float32
BF16 = jnp.bfloat16
VMEM = pl.BlockSpec(memory_space=pltpu.VMEM)
SMEM = pl.BlockSpec(memory_space=pltpu.SMEM)
LIMIT = 32 * 1024 * 1024


def wave_table():
    rows = []
    tiles = np.arange(N_TILE)
    for rho in ORDER:
        k = np.concatenate([16 * tiles + 8 * kk + rho for kk in range(2)])
        m = (k[:, None] * np.arange(SPAN)[None, :]) % NPIX
        angle = 2.0 * np.pi * m / NPIX
        rows += [np.cos(angle), -np.sin(angle)]
    return np.concatenate(rows).astype(ml_dtypes.bfloat16)


def order_matrix():
    out = np.zeros((2 * KMAX, 2 * KMAX), np.float32)
    for place, rho in enumerate(ORDER):
        for sign in range(2):
            for kk in range(2):
                for t in range(N_TILE):
                    j = 16 * t + 8 * kk + rho
                    q = KMAX + j if sign == 0 else (KMAX - j if j else 0)
                    out[q, place * LANES + sign * 64 + kk * N_TILE + t] = 1.0
    return out.astype(ml_dtypes.bfloat16)


def edge_waves():
    step = lax.broadcasted_iota(jnp.int32, (1, SPAN), 1) & 7
    diag = jnp.where(step & 1 == 1, HALF, 1.0)
    cos = jnp.where(step & 3 == 2, 0.0, jnp.where((step >= 3) & (step <= 5), -diag, diag))
    sin = jnp.where(step & 3 == 0, 0.0, jnp.where(step >= 5, -diag, diag))
    return cos.astype(F32), sin.astype(F32)


def dft4(x, sign):
    (r0, i0), (r1, i1), (r2, i2), (r3, i3) = x
    ar, ai, br, bi = r0 + r2, i0 + i2, r0 - r2, i0 - i2
    cr, ci, dr, di = r1 + r3, i1 + i3, r1 - r3, i1 - i3
    if sign < 0:
        dr, di = -dr, -di
    return [(ar + cr, ai + ci), (br - di, bi + dr), (ar - cr, ai - ci), (br + di, bi - dr)]


def dft8(x, sign):
    even = dft4(x[0::2], sign)
    odd = dft4(x[1::2], sign)
    (r1, i1), (r2, i2), (r3, i3) = odd[1:]
    if sign > 0:
        turned = [odd[0], (HALF * (r1 - i1), HALF * (r1 + i1)), (-i2, r2), (-HALF * (r3 + i3), HALF * (r3 - i3))]
    else:
        turned = [odd[0], (HALF * (r1 + i1), HALF * (i1 - r1)), (i2, -r2), (HALF * (i3 - r3), -HALF * (r3 + i3))]
    low = [(a + c, b + d) for (a, b), (c, d) in zip(even, turned)]
    high = [(a - c, b - d) for (a, b), (c, d) in zip(even, turned)]
    return low + high


def dot_nt(a, b):
    return lax.dot_general(a, b, (((1,), (1,)), ((), ())), preferred_element_type=F32)


def dot_nn(a, b):
    return lax.dot_general(a, b, (((1,), (0,)), ((), ())), preferred_element_type=F32)


def dot_tn(a, b):
    return lax.dot_general(a, b, (((0,), (0,)), ((), ())), preferred_element_type=F32)


def table_of(table_ref, *rhos):
    start = PLACE[rhos[0]] * LANES
    return table_ref[start : start + LANES * len(rhos), :]


def columns_kernel(
    weight_ref, slab_ref, table_ref, out_ref, cells_ref, held_ref, fold_ref, band_ref,
    scale_ref, sems, table_sem, scale_sem,
):
    def fetch(chunk):
        rows = pl.ds(chunk * CHUNK, CHUNK)
        return pltpu.make_async_copy(slab_ref.at[0, :, rows, :], cells_ref.at[chunk], sems.at[chunk])

    def fetch_table():
        return pltpu.make_async_copy(table_ref, held_ref, table_sem)

    for chunk in range(CHUNKS):
        fetch(chunk).start(priority=chunk % 2)
    scales = pltpu.make_async_copy(weight_ref, scale_ref, scale_sem)
    scales.start()
    fetch_table().start()
    scales.wait()
    weights = [scale_ref[0, layer] for layer in range(slab_ref.shape[1])]

    def butterfly(chunk, start):
        def segment(m):
            cols = slice(m * SPAN + start, m * SPAN + start + LANES)
            total = cells_ref[chunk, 0, :, cols].astype(F32) * weights[0]
            for layer in range(1, len(weights)):
                total = total + cells_ref[chunk, layer, :, cols].astype(F32) * weights[layer]
            return total

        def keep(index, value):
            fold_ref[index, chunk * CHUNK : (chunk + 1) * CHUNK, start : start + LANES] = value.astype(BF16)

        x0, x4 = segment(0), segment(4)
        a0, a1 = x0 + x4, x0 - x4
        x2, x6 = segment(2), segment(6)
        a2, a3 = x2 + x6, x2 - x6
        x1, x5 = segment(1), segment(5)
        b0, b1 = x1 + x5, x1 - x5
        x3, x7 = segment(3), segment(7)
        b2, b3 = x3 + x7, x3 - x7
        total, other = a0 + a2, b0 + b2
        keep(0, total + other)
        keep(1, total - other)
        minus, plus = HALF * (b1 - b3), HALF * (b1 + b3)
        keep(2, a1 + minus)
        keep(3, -a3 - plus)
        keep(4, a0 - a2)
        keep(5, b2 - b0)
        keep(6, a1 - minus)
        keep(7, a3 - plus)

    for chunk in range(CHUNKS):
        fetch(chunk).wait()
        for start in range(0, SPAN, LANES):
            butterfly(chunk, start)
    fetch_table().wait()

    def place(rho, re, im):
        for s, part in enumerate((re, im)):
            for kk in range(2):
                start = 16 * s + 8 * kk + rho
                band_ref[pl.ds(start, N_TILE, stride=32), :] = part[kk * N_TILE : (kk + 1) * N_TILE]

    for rho in (0, 4):
        got = dot_nt(table_of(held_ref, rho), fold_ref[PLACE[rho]])
        place(rho, got[:64], got[64:])
    for number, (rho, back) in enumerate(DUOS):
        pair = fold_ref[2 + 2 * number : 4 + 2 * number].reshape(2 * ROWS, SPAN)
        got = dot_nt(table_of(held_ref, rho, back), pair)
        cu, cv = got[:64, :ROWS], got[:64, ROWS:]
        su, sv = got[64:128, :ROWS], got[64:128, ROWS:]
        place(rho, cu - sv, cv + su)
        cu, cv = got[128:192, :ROWS], got[128:192, ROWS:]
        su, sv = got[192:, :ROWS], got[192:, ROWS:]
        place(back, cu + sv, su - cv)
    out_ref[...] = band_ref[...].astype(BF16)


def columns(slab, weight, table):
    hbm = pl.BlockSpec(memory_space=pltpu.HBM)
    return pl.pallas_call(
        columns_kernel,
        in_specs=[hbm] * 3,
        out_specs=VMEM,
        out_shape=jax.ShapeDtypeStruct((2 * KMAX, ROWS), BF16),
        scratch_shapes=[
            pltpu.VMEM((CHUNKS, slab.shape[1], CHUNK, NPIX), BF16),
            pltpu.VMEM(table.shape, BF16),
            pltpu.VMEM((RADIX, ROWS, SPAN), BF16),
            pltpu.VMEM((2 * KMAX, ROWS), F32),
            pltpu.SMEM(weight.shape, F32),
            pltpu.SemaphoreType.DMA((CHUNKS,)),
            pltpu.SemaphoreType.DMA,
            pltpu.SemaphoreType.DMA,
        ],
        compiler_params=pltpu.CompilerParams(vmem_limit_bytes=60 * 1024 * 1024),
        name="columns",
    )(weight, slab, table)


def kernel_value(index_ref, values_ref, b, p):
    return values_ref[index_ref[b, p]]


def rows_kernel(band_ref, table_ref, ell_ref, out_ref, fold_ref):
    cos, sin = edge_waves()
    edge_re = jnp.zeros((16, 1), F32)
    edge_im = jnp.zeros((16, 1), F32)
    for u in range(SPAN // LANES):
        cols = slice(u * LANES, (u + 1) * LANES)
        starts = [(4 * m + u) * 32 for m in range(RADIX)]
        parts = [
            tuple(band_ref[start + 16 * s : start + 16 * s + 16, :].astype(F32) for s in range(2))
            for start in starts
        ]
        folded = dft8(parts, -1)
        for rho, (re, im) in enumerate(folded):
            fold_ref[PLACE[rho], 0:16, cols] = re.astype(BF16)
            fold_ref[PLACE[rho], 16:32, cols] = im.astype(BF16)
        up, vp = folded[0]
        edge_re = edge_re + jnp.sum(up * cos[:, cols] - vp * sin[:, cols], axis=1, keepdims=True)
        edge_im = edge_im + jnp.sum(vp * cos[:, cols] + up * sin[:, cols], axis=1, keepdims=True)
    lane = lax.broadcasted_iota(jnp.int32, (16, LANES), 1)
    low = lane < 64

    def lines(ahead, back):
        (cu, cv), (du, dv) = ahead, back
        real = jnp.where(low, cu - pltpu.roll(cv, 64, 1), pltpu.roll(du, 64, 1) + dv)
        imag = jnp.where(low, cv + pltpu.roll(cu, 64, 1), pltpu.roll(dv, 64, 1) - du)
        return real, imag

    def keep(rho, real, imag):
        cols = slice(PLACE[rho] * LANES, (PLACE[rho] + 1) * LANES)
        out_ref[0:16, cols] = real.astype(BF16)
        out_ref[16:32, cols] = imag.astype(BF16)

    for rho in (0, 4):
        got = dot_nt(fold_ref[PLACE[rho]], table_of(table_ref, rho))
        both = (got[:16], got[16:])
        real, imag = lines(both, both)
        if rho == 0:
            real = jnp.where(lane == 64, edge_re, real)
            imag = jnp.where(lane == 64, edge_im, imag)
        keep(rho, real, imag)
    for rho, back in DUOS:
        four = fold_ref[PLACE[rho] : PLACE[rho] + 2].reshape(64, SPAN)
        got = dot_nt(four, table_of(table_ref, rho, back))
        for place, one in enumerate((rho, back)):
            part = got[:, place * LANES : (place + 1) * LANES]
            duo = ((part[0:16], part[16:32]), (part[32:48], part[48:64]))
            keep(one, *lines(duo[place], duo[1 - place]))
    bins = ell_ref[...].astype(F32).astype(BF16)
    out_ref[0:16, 2 * KMAX :] = bins
    out_ref[16:32, 2 * KMAX :] = bins


def rows(band, table, ell):
    return pl.pallas_call(
        rows_kernel,
        in_specs=[VMEM, VMEM, VMEM],
        out_specs=VMEM,
        out_shape=jax.ShapeDtypeStruct((32, WIDTH), BF16),
        scratch_shapes=[pltpu.VMEM((RADIX, 32, SPAN), BF16)],
        compiler_params=pltpu.CompilerParams(vmem_limit_bytes=LIMIT),
        name="rows",
    )(band, table, ell)


def modes_kernel(
    plane_ref, index_ref, values_ref, near_ref, far1_ref, far2_ref, far3_ref, order_ref,
    kappa_ref, sums_ref, ell_ref, lines_ref, terms_ref,
):
    plane = plane_ref[0]
    for number, ref in enumerate((near_ref, far1_ref, far2_ref, far3_ref)):
        for slot in range(2):
            lines_ref[plane ^ (2 * number + slot)] = ref[slot]
    bins = jnp.concatenate([lines_ref[p, 0:16, 2 * KMAX :] for p in range(N_PLANE)], axis=1)
    ell_ref[...] = dot_nn(bins, order_ref[...]).astype(jnp.int32)
    weights = [[kernel_value(index_ref, values_ref, b, p) for p in range(N_PLANE)] for b in range(BINS)]
    for tile in range(RADIX):
        cols = slice(tile * LANES, (tile + 1) * LANES)
        kappa = [None] * BINS
        for p in range(N_PLANE):
            line = lines_ref[p, :, cols].astype(F32)
            for b in range(BINS):
                term = line * weights[b][p]
                kappa[b] = term if p == 0 else kappa[b] + term
        for b in range(BINS):
            kappa_ref[32 * b : 32 * b + 32, cols] = kappa[b]
        for number, (i, j) in enumerate(FIRST_GROUP + SECOND_GROUP):
            both = kappa[i] * kappa[j]
            terms_ref[number, :, cols] = both[0:16] + both[16:32]

    lane = lax.broadcasted_iota(jnp.int32, (8, LANES), 1)
    sub = lax.broadcasted_iota(jnp.int32, (8, LANES), 0)
    spread = [jnp.zeros((8, LANES), F32), jnp.zeros((8, LANES), F32)]
    for ell in range(ELLS):
        here = ell_ref[...] == ell
        held = [jnp.zeros((8, LANES), F32), jnp.zeros((8, LANES), F32)]
        for number in range(PAIRS):
            chosen = jnp.where(here, terms_ref[number], 0.0)
            chosen = chosen[0:8] + chosen[8:16]
            total = chosen[:, 0:LANES]
            for tile in range(1, RADIX):
                total = total + chosen[:, tile * LANES : (tile + 1) * LANES]
            total = jnp.sum(total, axis=0, keepdims=True)
            group, row = divmod(number, 8)
            held[group] = jnp.where(sub == row, total, held[group])
        for group in range(2):
            total = jnp.sum(held[group], axis=1, keepdims=True)
            spread[group] = jnp.where(lane & 15 == ell, total, spread[group])
    own = (lane >> 4) == sub
    sums = [jnp.sum(jnp.where(own, part, 0.0), axis=0, keepdims=True) for part in spread]
    pattern = jnp.where(sub & 1 == 0, sums[0], sums[1])
    sums_ref[...] = jnp.broadcast_to(pattern[None], (N_TILE // 4, 8, LANES)).reshape(2 * N_TILE, LANES)


def modes(plane, index, values, near, far, order):
    return pl.pallas_call(
        modes_kernel,
        in_specs=[SMEM, SMEM, SMEM] + [VMEM] * 5,
        out_specs=[VMEM, VMEM, VMEM],
        out_shape=[
            jax.ShapeDtypeStruct((32 * BINS, 2 * KMAX), F32),
            jax.ShapeDtypeStruct((2 * N_TILE, LANES), F32),
            jax.ShapeDtypeStruct((16, 2 * KMAX), jnp.int32),
        ],
        scratch_shapes=[
            pltpu.VMEM((N_PLANE, 32, WIDTH), BF16),
            pltpu.VMEM((PAIRS, 16, 2 * KMAX), F32),
        ],
        compiler_params=pltpu.CompilerParams(vmem_limit_bytes=LIMIT),
        name="modes",
    )(plane, index, values, near, *far, order)


def adjoint_kernel(
    plane_ref, index_ref, values_ref, sums_ref, kappa_ref, ell_ref, target_ref, table_ref,
    spectra_ref, out_ref, weight_ref, line_ref, spread_ref,
):
    total = jnp.sum(sums_ref[...].reshape(N_TILE // 4, 8, LANES), axis=0)
    total = total + pltpu.roll(total, 2, 0)
    total = total + pltpu.roll(total, 4, 0)
    lane = lax.broadcasted_iota(jnp.int32, (1, LANES), 1)
    area = (2.0 * lane.astype(F32) + 1.0) * (float((KMAX // ELLS) ** 2) * (0.5 * math.pi))
    scale = float(NPIX * NPIX) * area
    for row, group in enumerate((FIRST_GROUP, SECOND_GROUP)):
        line = total[row : row + 1, :]
        for place, pair in enumerate(group):
            turned = line if place == 0 else pltpu.roll(line, LANES - 16 * place, 1)
            number = PAIR_ID[pair]
            spectra_ref[number : number + 1, :] = (turned / scale)[:, :ELLS]
    weight_ref[...] = jnp.zeros_like(weight_ref)
    weight_ref[0:10, 0:ELLS] = (spectra_ref[...] - target_ref[...]) * (
        float(KMAX) / (ELLS * NPIX)
    ) / area[:, :ELLS]

    couplings = []
    for number in range(PAIRS):
        row = weight_ref[number : number + 1, :]
        row = row + row if number in (PAIR_ID[(i, i)] for i in range(BINS)) else row
        couplings.append(jnp.broadcast_to(row, (8, LANES)))
    plane = plane_ref[0]
    weights = [kernel_value(index_ref, values_ref, b, plane) for b in range(BINS)]

    for tile in range(RADIX):
        cols = slice(tile * LANES, (tile + 1) * LANES)
        for half in range(0, 16, 8):
            where = ell_ref[half : half + 8, cols]
            mixers = [jnp.take_along_axis(table, where, axis=1) for table in couplings]
            for s in range(2):
                start = 16 * s + half
                kappa = [kappa_ref[32 * b + start : 32 * b + start + 8, cols] for b in range(BINS)]
                line = None
                for i in range(BINS):
                    grad = mixers[PAIR_ID[(i, 0)]] * kappa[0]
                    for j in range(1, BINS):
                        grad = grad + mixers[PAIR_ID[(i, j)]] * kappa[j]
                    term = grad.astype(BF16).astype(F32) * weights[i]
                    line = term if i == 0 else line + term
                line_ref[start : start + 8, cols] = line

    wide_lane = lax.broadcasted_iota(jnp.int32, (16, LANES), 1)
    low = wide_lane < 64

    def factors(rho):
        cols = slice(PLACE[rho] * LANES, (PLACE[rho] + 1) * LANES)
        g0, g1 = line_ref[0:16, cols], line_ref[16:32, cols]
        if rho == 0:
            g0 = jnp.where(wide_lane == 64, 0.0, g0)
            g1 = jnp.where(wide_lane == 64, 0.0, g1)
        t0, t1 = pltpu.roll(g0, 64, 1), pltpu.roll(g1, 64, 1)
        ahead = (jnp.where(low, g0, t1), jnp.where(low, g1, -t0))
        back = (jnp.where(low, t0, -g1), jnp.where(low, t1, g0))
        return ahead, back

    def spread(rho, re, im):
        spread_ref[2 * rho] = re
        spread_ref[2 * rho + 1] = im

    start = PLACE[0] * LANES + 64
    edge0 = line_ref[0:16, start : start + 1]
    edge1 = line_ref[16:32, start : start + 1]
    cos, sin = edge_waves()
    for rho in (0, 4):
        ahead, back = factors(rho)
        left = jnp.concatenate([ahead[0] + back[0], ahead[1] + back[1]], axis=0).astype(BF16)
        got = dot_nn(left, table_of(table_ref, rho))
        re, im = got[:16], got[16:]
        if rho == 0:
            re = re + edge0 * cos + edge1 * sin
            im = im + edge1 * cos - edge0 * sin
        spread(rho, re, im)
    for rho, back in DUOS:
        plus, minus = factors(rho)
        plus_back, minus_back = factors(back)
        left = jnp.concatenate(
            [
                jnp.concatenate(plus + minus, axis=0),
                jnp.concatenate(minus_back + plus_back, axis=0),
            ],
            axis=1,
        ).astype(BF16)
        got = dot_nn(left, table_of(table_ref, rho, back))
        spread(rho, got[0:16], got[16:32])
        spread(back, got[32:48], got[48:64])
    for u in range(SPAN // LANES):
        cols = slice(u * LANES, (u + 1) * LANES)
        parts = [(spread_ref[2 * rho, :, cols], spread_ref[2 * rho + 1, :, cols]) for rho in range(RADIX)]
        for m, both in enumerate(dft8(parts, 1)):
            for s in range(2):
                begin = (4 * m + u) * 32 + 16 * s
                out_ref[begin : begin + 16, :] = both[s].astype(BF16)


def adjoint(plane, index, values, sums, kappa, ell, target, table):
    return pl.pallas_call(
        adjoint_kernel,
        in_specs=[SMEM, SMEM, SMEM, VMEM, VMEM, VMEM, VMEM, VMEM],
        out_specs=[VMEM, VMEM],
        out_shape=[
            jax.ShapeDtypeStruct(target.shape, F32),
            jax.ShapeDtypeStruct((2 * KMAX, ROWS), BF16),
        ],
        scratch_shapes=[
            pltpu.VMEM((16, LANES), F32),
            pltpu.VMEM((32, 2 * KMAX), F32),
            pltpu.VMEM((2 * RADIX, 16, SPAN), F32),
        ],
        compiler_params=pltpu.CompilerParams(vmem_limit_bytes=LIMIT),
        name="adjoint",
    )(plane, index, values, sums, kappa, ell, target, table)


def maps_kernel(band_ref, table_ref, out_ref, wide_ref):
    wide_ref[...] = band_ref[...].astype(F32)

    def block(rho, s):
        parts = [
            wide_ref[pl.ds(16 * s + 8 * kk + rho, N_TILE, stride=32), :] for kk in range(2)
        ]
        return jnp.concatenate(parts, axis=0)

    flat = []
    for rho in (0, 4):
        left = jnp.concatenate([block(rho, 0), block(rho, 1)], axis=0).astype(BF16)
        flat.append(dot_tn(left, table_of(table_ref, rho)))
    p, q = [None], [None]
    for rho, back in DUOS:
        b0, b1, e0, e1 = block(rho, 0), block(rho, 1), block(back, 0), block(back, 1)
        left = jnp.concatenate(
            [
                jnp.concatenate([b0, b1, e0, e1], axis=0),
                jnp.concatenate([b1, -b0, -e1, e0], axis=0),
            ],
            axis=1,
        ).astype(BF16)
        got = dot_tn(left, table_of(table_ref, rho, back))
        p.append(got[:ROWS])
        q.append(got[ROWS:])
    plus, minus = flat[0] + flat[1], flat[0] - flat[1]

    def put(m, even, odd):
        out_ref[0, :, m * SPAN : (m + 1) * SPAN] = even + odd
        out_ref[0, :, (m + 4) * SPAN : (m + 5) * SPAN] = even - odd

    put(0, plus + p[2], p[1] + p[3])
    put(1, minus - q[2], HALF * (p[1] - q[1] - p[3] - q[3]))
    put(2, plus - p[2], q[3] - q[1])
    put(3, minus + q[2], HALF * (p[3] - p[1] - q[1] - q[3]))


def maps(band, table):
    return pl.pallas_call(
        maps_kernel,
        in_specs=[VMEM, VMEM],
        out_specs=VMEM,
        out_shape=jax.ShapeDtypeStruct((1, ROWS, NPIX), F32),
        scratch_shapes=[pltpu.VMEM((2 * KMAX, ROWS), F32)],
        compiler_params=pltpu.CompilerParams(vmem_limit_bytes=LIMIT),
        name="maps",
    )(band, table)


def body(slab_cells, slab_weight, kernel_table, kernel_index, ell_index, target_spectra):
    table = jnp.asarray(wave_table())
    order = jnp.asarray(order_matrix())
    exchange = functools.partial(
        lax.all_to_all, axis_name="tile", split_axis=0, concat_axis=0, tiled=True
    )

    def swap(value, bits):
        return lax.ppermute(value, "plane", [(p, p ^ bits) for p in range(N_PLANE)])

    plane = lax.axis_index("plane").astype(jnp.int32).reshape(1)
    band = exchange(columns(slab_cells, slab_weight, table))
    lines = rows(band, table, ell_index.T)
    near = jnp.stack([lines, swap(lines, 1)])
    far = [swap(near, bits) for bits in (2, 4, 6)]
    kappa, sums, ell = modes(plane, kernel_index, kernel_table, near, far, order)
    spectra, adjoint_band = adjoint(
        plane, kernel_index, kernel_table, exchange(sums), kappa, ell, target_spectra, table
    )
    return spectra, maps(exchange(adjoint_band), table)


def solution(mesh):
    return jax.shard_map(
        body,
        mesh=mesh,
        in_specs=(
            P("plane", None, "tile", None),
            P("plane", None),
            P(),
            P(),
            P("plane", "tile"),
            P(),
        ),
        out_specs=(P(), P("plane", "tile", None)),
        check_vma=False,
    )
```

```python
import functools
import math

import jax
import jax.numpy as jnp
import ml_dtypes
import numpy as np
from jax import lax
from jax.experimental import pallas as pl
from jax.experimental.pallas import tpu as pltpu
from jax.sharding import PartitionSpec as P

NPIX = 4096
KMAX = 512
BINS = 4
ELLS = 16
RADIX = 8
SPAN = NPIX // RADIX
N_PLANE = 8
N_TILE = 32
ROWS = NPIX // N_TILE
LANES = 128
CHUNK = 16
WIDTH = 2 * KMAX + ROWS
PAIRS = BINS * (BINS + 1) // 2
CHUNKS = ROWS // CHUNK

ORDER = (0, 4, 1, 7, 2, 6, 3, 5)
PLACE = {rho: place for place, rho in enumerate(ORDER)}
DUOS = ((1, 7), (2, 6), (3, 5))
HALF = math.sqrt(0.5)

PAIR_ID = {}
for _number, (_i, _j) in enumerate(zip(*np.triu_indices(BINS))):
    PAIR_ID[(int(_i), int(_j))] = PAIR_ID[(int(_j), int(_i))] = _number
FIRST_GROUP = ((0, 0), (1, 1), (2, 2), (3, 3), (0, 1), (1, 2), (2, 3), (3, 0))
SECOND_GROUP = ((0, 2), (1, 3))

F32 = jnp.float32
BF16 = jnp.bfloat16
VMEM = pl.BlockSpec(memory_space=pltpu.VMEM)
SMEM = pl.BlockSpec(memory_space=pltpu.SMEM)
LIMIT = 32 * 1024 * 1024


def wave_table():
    rows = []
    tiles = np.arange(N_TILE)
    for rho in ORDER:
        k = np.concatenate([16 * tiles + 8 * kk + rho for kk in range(2)])
        m = (k[:, None] * np.arange(SPAN)[None, :]) % NPIX
        angle = 2.0 * np.pi * m / NPIX
        rows += [np.cos(angle), -np.sin(angle)]
    return np.concatenate(rows).astype(ml_dtypes.bfloat16)


def order_matrix():
    out = np.zeros((2 * KMAX, 2 * KMAX), np.float32)
    for place, rho in enumerate(ORDER):
        for sign in range(2):
            for kk in range(2):
                for t in range(N_TILE):
                    j = 16 * t + 8 * kk + rho
                    q = KMAX + j if sign == 0 else (KMAX - j if j else 0)
                    out[q, place * LANES + sign * 64 + kk * N_TILE + t] = 1.0
    return out.astype(ml_dtypes.bfloat16)


def edge_waves():
    step = lax.broadcasted_iota(jnp.int32, (1, SPAN), 1) & 7
    diag = jnp.where(step & 1 == 1, HALF, 1.0)
    cos = jnp.where(step & 3 == 2, 0.0, jnp.where((step >= 3) & (step <= 5), -diag, diag))
    sin = jnp.where(step & 3 == 0, 0.0, jnp.where(step >= 5, -diag, diag))
    return cos.astype(F32), sin.astype(F32)


def dft4(x, sign):
    (r0, i0), (r1, i1), (r2, i2), (r3, i3) = x
    ar, ai, br, bi = r0 + r2, i0 + i2, r0 - r2, i0 - i2
    cr, ci, dr, di = r1 + r3, i1 + i3, r1 - r3, i1 - i3
    if sign < 0:
        dr, di = -dr, -di
    return [(ar + cr, ai + ci), (br - di, bi + dr), (ar - cr, ai - ci), (br + di, bi - dr)]


def dft8(x, sign):
    even = dft4(x[0::2], sign)
    odd = dft4(x[1::2], sign)
    (r1, i1), (r2, i2), (r3, i3) = odd[1:]
    if sign > 0:
        turned = [odd[0], (HALF * (r1 - i1), HALF * (r1 + i1)), (-i2, r2), (-HALF * (r3 + i3), HALF * (r3 - i3))]
    else:
        turned = [odd[0], (HALF * (r1 + i1), HALF * (i1 - r1)), (i2, -r2), (HALF * (i3 - r3), -HALF * (r3 + i3))]
    low = [(a + c, b + d) for (a, b), (c, d) in zip(even, turned)]
    high = [(a - c, b - d) for (a, b), (c, d) in zip(even, turned)]
    return low + high


def dot_nt(a, b):
    return lax.dot_general(a, b, (((1,), (1,)), ((), ())), preferred_element_type=F32)


def dot_nn(a, b):
    return lax.dot_general(a, b, (((1,), (0,)), ((), ())), preferred_element_type=F32)


def dot_tn(a, b):
    return lax.dot_general(a, b, (((0,), (0,)), ((), ())), preferred_element_type=F32)


def table_of(table_ref, *rhos):
    start = PLACE[rhos[0]] * LANES
    return table_ref[start : start + LANES * len(rhos), :]


def columns_kernel(
    weight_ref, slab_ref, table_ref, out_ref, cells_ref, held_ref, fold_ref, band_ref,
    scale_ref, sems, table_sem, scale_sem,
):
    def fetch(chunk):
        rows = pl.ds(chunk * CHUNK, CHUNK)
        return pltpu.make_async_copy(slab_ref.at[0, :, rows, :], cells_ref.at[chunk], sems.at[chunk])

    def fetch_table():
        return pltpu.make_async_copy(table_ref, held_ref, table_sem)

    for chunk in range(CHUNKS):
        fetch(chunk).start(priority=chunk % 2)
    scales = pltpu.make_async_copy(weight_ref, scale_ref, scale_sem)
    scales.start()
    fetch_table().start()
    scales.wait()
    weights = [scale_ref[0, layer] for layer in range(slab_ref.shape[1])]

    def butterfly(chunk, start):
        def segment(m):
            cols = slice(m * SPAN + start, m * SPAN + start + LANES)
            total = cells_ref[chunk, 0, :, cols].astype(F32) * weights[0]
            for layer in range(1, len(weights)):
                total = total + cells_ref[chunk, layer, :, cols].astype(F32) * weights[layer]
            return total

        def keep(index, value):
            fold_ref[index, chunk * CHUNK : (chunk + 1) * CHUNK, start : start + LANES] = value.astype(BF16)

        x0, x4 = segment(0), segment(4)
        a0, a1 = x0 + x4, x0 - x4
        x2, x6 = segment(2), segment(6)
        a2, a3 = x2 + x6, x2 - x6
        x1, x5 = segment(1), segment(5)
        b0, b1 = x1 + x5, x1 - x5
        x3, x7 = segment(3), segment(7)
        b2, b3 = x3 + x7, x3 - x7
        total, other = a0 + a2, b0 + b2
        keep(0, total + other)
        keep(1, total - other)
        minus, plus = HALF * (b1 - b3), HALF * (b1 + b3)
        keep(2, a1 + minus)
        keep(3, -a3 - plus)
        keep(4, a0 - a2)
        keep(5, b2 - b0)
        keep(6, a1 - minus)
        keep(7, a3 - plus)

    for chunk in range(CHUNKS):
        fetch(chunk).wait()
        for start in range(0, SPAN, LANES):
            butterfly(chunk, start)
    fetch_table().wait()

    def place(rho, re, im):
        for s, part in enumerate((re, im)):
            for kk in range(2):
                start = 16 * s + 8 * kk + rho
                band_ref[pl.ds(start, N_TILE, stride=32), :] = part[kk * N_TILE : (kk + 1) * N_TILE]

    for rho in (0, 4):
        got = dot_nt(table_of(held_ref, rho), fold_ref[PLACE[rho]])
        place(rho, got[:64], got[64:])
    for number, (rho, back) in enumerate(DUOS):
        pair = fold_ref[2 + 2 * number : 4 + 2 * number].reshape(2 * ROWS, SPAN)
        got = dot_nt(table_of(held_ref, rho, back), pair)
        cu, cv = got[:64, :ROWS], got[:64, ROWS:]
        su, sv = got[64:128, :ROWS], got[64:128, ROWS:]
        place(rho, cu - sv, cv + su)
        cu, cv = got[128:192, :ROWS], got[128:192, ROWS:]
        su, sv = got[192:, :ROWS], got[192:, ROWS:]
        place(back, cu + sv, su - cv)
    out_ref[...] = band_ref[...].astype(BF16)


def columns(slab, weight, table):
    hbm = pl.BlockSpec(memory_space=pltpu.HBM)
    return pl.pallas_call(
        columns_kernel,
        in_specs=[hbm] * 3,
        out_specs=VMEM,
        out_shape=jax.ShapeDtypeStruct((2 * KMAX, ROWS), BF16),
        scratch_shapes=[
            pltpu.VMEM((CHUNKS, slab.shape[1], CHUNK, NPIX), BF16),
            pltpu.VMEM(table.shape, BF16),
            pltpu.VMEM((RADIX, ROWS, SPAN), BF16),
            pltpu.VMEM((2 * KMAX, ROWS), F32),
            pltpu.SMEM(weight.shape, F32),
            pltpu.SemaphoreType.DMA((CHUNKS,)),
            pltpu.SemaphoreType.DMA,
            pltpu.SemaphoreType.DMA,
        ],
        compiler_params=pltpu.CompilerParams(vmem_limit_bytes=60 * 1024 * 1024),
        name="columns",
    )(weight, slab, table)


def kernel_value(index_ref, values_ref, b, p):
    return values_ref[index_ref[b, p]]


def rows_kernel(band_ref, table_ref, ell_ref, out_ref, fold_ref):
    cos, sin = edge_waves()
    edge_re = jnp.zeros((16, 1), F32)
    edge_im = jnp.zeros((16, 1), F32)
    for u in range(SPAN // LANES):
        cols = slice(u * LANES, (u + 1) * LANES)
        starts = [(4 * m + u) * 32 for m in range(RADIX)]
        parts = [
            tuple(band_ref[start + 16 * s : start + 16 * s + 16, :].astype(F32) for s in range(2))
            for start in starts
        ]
        folded = dft8(parts, -1)
        for rho, (re, im) in enumerate(folded):
            fold_ref[PLACE[rho], 0:16, cols] = re.astype(BF16)
            fold_ref[PLACE[rho], 16:32, cols] = im.astype(BF16)
        up, vp = folded[0]
        edge_re = edge_re + jnp.sum(up * cos[:, cols] - vp * sin[:, cols], axis=1, keepdims=True)
        edge_im = edge_im + jnp.sum(vp * cos[:, cols] + up * sin[:, cols], axis=1, keepdims=True)
    lane = lax.broadcasted_iota(jnp.int32, (16, LANES), 1)
    low = lane < 64

    def lines(ahead, back):
        (cu, cv), (du, dv) = ahead, back
        real = jnp.where(low, cu - pltpu.roll(cv, 64, 1), pltpu.roll(du, 64, 1) + dv)
        imag = jnp.where(low, cv + pltpu.roll(cu, 64, 1), pltpu.roll(dv, 64, 1) - du)
        return real, imag

    def keep(rho, real, imag):
        cols = slice(PLACE[rho] * LANES, (PLACE[rho] + 1) * LANES)
        out_ref[0:16, cols] = real.astype(BF16)
        out_ref[16:32, cols] = imag.astype(BF16)

    for rho in (0, 4):
        got = dot_nt(fold_ref[PLACE[rho]], table_of(table_ref, rho))
        both = (got[:16], got[16:])
        real, imag = lines(both, both)
        if rho == 0:
            real = jnp.where(lane == 64, edge_re, real)
            imag = jnp.where(lane == 64, edge_im, imag)
        keep(rho, real, imag)
    for rho, back in DUOS:
        four = fold_ref[PLACE[rho] : PLACE[rho] + 2].reshape(64, SPAN)
        got = dot_nt(four, table_of(table_ref, rho, back))
        for place, one in enumerate((rho, back)):
            part = got[:, place * LANES : (place + 1) * LANES]
            duo = ((part[0:16], part[16:32]), (part[32:48], part[48:64]))
            keep(one, *lines(duo[place], duo[1 - place]))
    bins = ell_ref[...].astype(F32).astype(BF16)
    out_ref[0:16, 2 * KMAX :] = bins
    out_ref[16:32, 2 * KMAX :] = bins


def rows(band, table, ell):
    return pl.pallas_call(
        rows_kernel,
        in_specs=[VMEM, VMEM, VMEM],
        out_specs=VMEM,
        out_shape=jax.ShapeDtypeStruct((32, WIDTH), BF16),
        scratch_shapes=[pltpu.VMEM((RADIX, 32, SPAN), BF16)],
        compiler_params=pltpu.CompilerParams(vmem_limit_bytes=LIMIT),
        name="rows",
    )(band, table, ell)


def modes_kernel(
    plane_ref, index_ref, values_ref, *refs,
):
    order_ref, kappa_ref, sums_ref, ell_ref, lines_ref, terms_ref = refs[N_PLANE:]
    plane = plane_ref[0]
    for ref, bits in zip(refs, (0, 1, 2, 4, 6, 3, 5, 7)):
        lines_ref[plane ^ bits] = ref[...]
    bins = jnp.concatenate([lines_ref[p, 0:16, 2 * KMAX :] for p in range(N_PLANE)], axis=1)
    ell_ref[...] = dot_nn(bins, order_ref[...]).astype(jnp.int32)
    weights = [[kernel_value(index_ref, values_ref, b, p) for p in range(N_PLANE)] for b in range(BINS)]
    for tile in range(RADIX):
        cols = slice(tile * LANES, (tile + 1) * LANES)
        kappa = [None] * BINS
        for p in range(N_PLANE):
            line = lines_ref[p, :, cols].astype(F32)
            for b in range(BINS):
                term = line * weights[b][p]
                kappa[b] = term if p == 0 else kappa[b] + term
        for b in range(BINS):
            kappa_ref[32 * b : 32 * b + 32, cols] = kappa[b]
        for number, (i, j) in enumerate(FIRST_GROUP + SECOND_GROUP):
            both = kappa[i] * kappa[j]
            terms_ref[number, :, cols] = both[0:16] + both[16:32]

    lane = lax.broadcasted_iota(jnp.int32, (8, LANES), 1)
    sub = lax.broadcasted_iota(jnp.int32, (8, LANES), 0)
    spread = [jnp.zeros((8, LANES), F32), jnp.zeros((8, LANES), F32)]
    for ell in range(ELLS):
        here = ell_ref[...] == ell
        held = [jnp.zeros((8, LANES), F32), jnp.zeros((8, LANES), F32)]
        for number in range(PAIRS):
            chosen = jnp.where(here, terms_ref[number], 0.0)
            chosen = chosen[0:8] + chosen[8:16]
            total = chosen[:, 0:LANES]
            for tile in range(1, RADIX):
                total = total + chosen[:, tile * LANES : (tile + 1) * LANES]
            total = jnp.sum(total, axis=0, keepdims=True)
            group, row = divmod(number, 8)
            held[group] = jnp.where(sub == row, total, held[group])
        for group in range(2):
            total = jnp.sum(held[group], axis=1, keepdims=True)
            spread[group] = jnp.where(lane & 15 == ell, total, spread[group])
    own = (lane >> 4) == sub
    sums = [jnp.sum(jnp.where(own, part, 0.0), axis=0, keepdims=True) for part in spread]
    pattern = jnp.where(sub & 1 == 0, sums[0], sums[1])
    sums_ref[...] = jnp.broadcast_to(pattern[None], (N_TILE // 4, 8, LANES)).reshape(2 * N_TILE, LANES)


def modes(plane, index, values, group, order):
    return pl.pallas_call(
        modes_kernel,
        in_specs=[SMEM, SMEM, SMEM] + [VMEM] * 9,
        out_specs=[VMEM, VMEM, VMEM],
        out_shape=[
            jax.ShapeDtypeStruct((32 * BINS, 2 * KMAX), F32),
            jax.ShapeDtypeStruct((2 * N_TILE, LANES), F32),
            jax.ShapeDtypeStruct((16, 2 * KMAX), jnp.int32),
        ],
        scratch_shapes=[
            pltpu.VMEM((N_PLANE, 32, WIDTH), BF16),
            pltpu.VMEM((PAIRS, 16, 2 * KMAX), F32),
        ],
        compiler_params=pltpu.CompilerParams(vmem_limit_bytes=LIMIT),
        name="modes",
    )(plane, index, values, *group, order)


def adjoint_kernel(
    plane_ref, index_ref, values_ref, sums_ref, kappa_ref, ell_ref, target_ref, table_ref,
    spectra_ref, out_ref, weight_ref, line_ref, spread_ref,
):
    total = jnp.sum(sums_ref[...].reshape(N_TILE // 4, 8, LANES), axis=0)
    total = total + pltpu.roll(total, 2, 0)
    total = total + pltpu.roll(total, 4, 0)
    lane = lax.broadcasted_iota(jnp.int32, (1, LANES), 1)
    area = (2.0 * lane.astype(F32) + 1.0) * (float((KMAX // ELLS) ** 2) * (0.5 * math.pi))
    scale = float(NPIX * NPIX) * area
    for row, group in enumerate((FIRST_GROUP, SECOND_GROUP)):
        line = total[row : row + 1, :]
        for place, pair in enumerate(group):
            turned = line if place == 0 else pltpu.roll(line, LANES - 16 * place, 1)
            number = PAIR_ID[pair]
            spectra_ref[number : number + 1, :] = (turned / scale)[:, :ELLS]
    weight_ref[...] = jnp.zeros_like(weight_ref)
    weight_ref[0:10, 0:ELLS] = (spectra_ref[...] - target_ref[...]) * (
        float(KMAX) / (ELLS * NPIX)
    ) / area[:, :ELLS]

    couplings = []
    for number in range(PAIRS):
        row = weight_ref[number : number + 1, :]
        row = row + row if number in (PAIR_ID[(i, i)] for i in range(BINS)) else row
        couplings.append(jnp.broadcast_to(row, (8, LANES)))
    plane = plane_ref[0]
    weights = [kernel_value(index_ref, values_ref, b, plane) for b in range(BINS)]

    for tile in range(RADIX):
        cols = slice(tile * LANES, (tile + 1) * LANES)
        for half in range(0, 16, 8):
            where = ell_ref[half : half + 8, cols]
            mixers = [jnp.take_along_axis(table, where, axis=1) for table in couplings]
            for s in range(2):
                start = 16 * s + half
                kappa = [kappa_ref[32 * b + start : 32 * b + start + 8, cols] for b in range(BINS)]
                line = None
                for i in range(BINS):
                    grad = mixers[PAIR_ID[(i, 0)]] * kappa[0]
                    for j in range(1, BINS):
                        grad = grad + mixers[PAIR_ID[(i, j)]] * kappa[j]
                    term = grad.astype(BF16).astype(F32) * weights[i]
                    line = term if i == 0 else line + term
                line_ref[start : start + 8, cols] = line

    wide_lane = lax.broadcasted_iota(jnp.int32, (16, LANES), 1)
    low = wide_lane < 64

    def factors(rho):
        cols = slice(PLACE[rho] * LANES, (PLACE[rho] + 1) * LANES)
        g0, g1 = line_ref[0:16, cols], line_ref[16:32, cols]
        if rho == 0:
            g0 = jnp.where(wide_lane == 64, 0.0, g0)
            g1 = jnp.where(wide_lane == 64, 0.0, g1)
        t0, t1 = pltpu.roll(g0, 64, 1), pltpu.roll(g1, 64, 1)
        ahead = (jnp.where(low, g0, t1), jnp.where(low, g1, -t0))
        back = (jnp.where(low, t0, -g1), jnp.where(low, t1, g0))
        return ahead, back

    def spread(rho, re, im):
        spread_ref[2 * rho] = re
        spread_ref[2 * rho + 1] = im

    start = PLACE[0] * LANES + 64
    edge0 = line_ref[0:16, start : start + 1]
    edge1 = line_ref[16:32, start : start + 1]
    cos, sin = edge_waves()
    for rho in (0, 4):
        ahead, back = factors(rho)
        left = jnp.concatenate([ahead[0] + back[0], ahead[1] + back[1]], axis=0).astype(BF16)
        got = dot_nn(left, table_of(table_ref, rho))
        re, im = got[:16], got[16:]
        if rho == 0:
            re = re + edge0 * cos + edge1 * sin
            im = im + edge1 * cos - edge0 * sin
        spread(rho, re, im)
    for rho, back in DUOS:
        plus, minus = factors(rho)
        plus_back, minus_back = factors(back)
        left = jnp.concatenate(
            [
                jnp.concatenate(plus + minus, axis=0),
                jnp.concatenate(minus_back + plus_back, axis=0),
            ],
            axis=1,
        ).astype(BF16)
        got = dot_nn(left, table_of(table_ref, rho, back))
        spread(rho, got[0:16], got[16:32])
        spread(back, got[32:48], got[48:64])
    for u in range(SPAN // LANES):
        cols = slice(u * LANES, (u + 1) * LANES)
        parts = [(spread_ref[2 * rho, :, cols], spread_ref[2 * rho + 1, :, cols]) for rho in range(RADIX)]
        for m, both in enumerate(dft8(parts, 1)):
            for s in range(2):
                begin = (4 * m + u) * 32 + 16 * s
                out_ref[begin : begin + 16, :] = both[s].astype(BF16)


def adjoint(plane, index, values, sums, kappa, ell, target, table):
    return pl.pallas_call(
        adjoint_kernel,
        in_specs=[SMEM, SMEM, SMEM, VMEM, VMEM, VMEM, VMEM, VMEM],
        out_specs=[VMEM, VMEM],
        out_shape=[
            jax.ShapeDtypeStruct(target.shape, F32),
            jax.ShapeDtypeStruct((2 * KMAX, ROWS), BF16),
        ],
        scratch_shapes=[
            pltpu.VMEM((16, LANES), F32),
            pltpu.VMEM((32, 2 * KMAX), F32),
            pltpu.VMEM((2 * RADIX, 16, SPAN), F32),
        ],
        compiler_params=pltpu.CompilerParams(vmem_limit_bytes=LIMIT),
        name="adjoint",
    )(plane, index, values, sums, kappa, ell, target, table)


def maps_kernel(band_ref, table_ref, out_ref, wide_ref):
    wide_ref[...] = band_ref[...].astype(F32)

    def block(rho, s):
        parts = [
            wide_ref[pl.ds(16 * s + 8 * kk + rho, N_TILE, stride=32), :] for kk in range(2)
        ]
        return jnp.concatenate(parts, axis=0)

    flat = []
    for rho in (0, 4):
        left = jnp.concatenate([block(rho, 0), block(rho, 1)], axis=0).astype(BF16)
        flat.append(dot_tn(left, table_of(table_ref, rho)))
    p, q = [None], [None]
    for rho, back in DUOS:
        b0, b1, e0, e1 = block(rho, 0), block(rho, 1), block(back, 0), block(back, 1)
        left = jnp.concatenate(
            [
                jnp.concatenate([b0, b1, e0, e1], axis=0),
                jnp.concatenate([b1, -b0, -e1, e0], axis=0),
            ],
            axis=1,
        ).astype(BF16)
        got = dot_tn(left, table_of(table_ref, rho, back))
        p.append(got[:ROWS])
        q.append(got[ROWS:])
    plus, minus = flat[0] + flat[1], flat[0] - flat[1]

    def put(m, even, odd):
        out_ref[0, :, m * SPAN : (m + 1) * SPAN] = even + odd
        out_ref[0, :, (m + 4) * SPAN : (m + 5) * SPAN] = even - odd

    put(0, plus + p[2], p[1] + p[3])
    put(1, minus - q[2], HALF * (p[1] - q[1] - p[3] - q[3]))
    put(2, plus - p[2], q[3] - q[1])
    put(3, minus + q[2], HALF * (p[3] - p[1] - q[1] - q[3]))


def maps(band, table):
    return pl.pallas_call(
        maps_kernel,
        in_specs=[VMEM, VMEM],
        out_specs=VMEM,
        out_shape=jax.ShapeDtypeStruct((1, ROWS, NPIX), F32),
        scratch_shapes=[pltpu.VMEM((2 * KMAX, ROWS), F32)],
        compiler_params=pltpu.CompilerParams(vmem_limit_bytes=LIMIT),
        name="maps",
    )(band, table)


def body(slab_cells, slab_weight, kernel_table, kernel_index, ell_index, target_spectra):
    table = jnp.asarray(wave_table())
    order = jnp.asarray(order_matrix())
    exchange = functools.partial(
        lax.all_to_all, axis_name="tile", split_axis=0, concat_axis=0, tiled=True
    )

    def swap(value, bits):
        return lax.ppermute(value, "plane", [(p, p ^ bits) for p in range(N_PLANE)])

    plane = lax.axis_index("plane").astype(jnp.int32).reshape(1)
    band = exchange(columns(slab_cells, slab_weight, table))
    lines = rows(band, table, ell_index.T)
    across = swap(lines, 1)
    group = [lines, across]
    for part in (lines, across):
        group += [swap(part, bits) for bits in (2, 4, 6)]
    kappa, sums, ell = modes(plane, kernel_index, kernel_table, group, order)
    spectra, adjoint_band = adjoint(
        plane, kernel_index, kernel_table, exchange(sums), kappa, ell, target_spectra, table
    )
    return spectra, maps(exchange(adjoint_band), table)


def solution(mesh):
    return jax.shard_map(
        body,
        mesh=mesh,
        in_specs=(
            P("plane", None, "tile", None),
            P("plane", None),
            P(),
            P(),
            P("plane", "tile"),
            P(),
        ),
        out_specs=(P(), P("plane", "tile", None)),
        check_vma=False,
    )
```

```python
import functools
import math

import jax
import jax.numpy as jnp
import ml_dtypes
import numpy as np
from jax import lax
from jax.experimental import pallas as pl
from jax.experimental.pallas import tpu as pltpu
from jax.sharding import PartitionSpec as P

NPIX = 4096
KMAX = 512
BINS = 4
ELLS = 16
RADIX = 8
SPAN = NPIX // RADIX
N_PLANE = 8
N_TILE = 32
ROWS = NPIX // N_TILE
LANES = 128
CHUNK = 16
WIDTH = 2 * KMAX + ROWS
PAIRS = BINS * (BINS + 1) // 2
CHUNKS = ROWS // CHUNK

ORDER = (0, 4, 1, 7, 2, 6, 3, 5)
PLACE = {rho: place for place, rho in enumerate(ORDER)}
DUOS = ((1, 7), (2, 6), (3, 5))
HALF = math.sqrt(0.5)

PAIR_ID = {}
for _number, (_i, _j) in enumerate(zip(*np.triu_indices(BINS))):
    PAIR_ID[(int(_i), int(_j))] = PAIR_ID[(int(_j), int(_i))] = _number
FIRST_GROUP = ((0, 0), (1, 1), (2, 2), (3, 3), (0, 1), (1, 2), (2, 3), (3, 0))
SECOND_GROUP = ((0, 2), (1, 3))

F32 = jnp.float32
BF16 = jnp.bfloat16
VMEM = pl.BlockSpec(memory_space=pltpu.VMEM)
SMEM = pl.BlockSpec(memory_space=pltpu.SMEM)
LIMIT = 32 * 1024 * 1024


def wave_table():
    rows = []
    tiles = np.arange(N_TILE)
    for rho in ORDER:
        k = np.concatenate([16 * tiles + 8 * kk + rho for kk in range(2)])
        m = (k[:, None] * np.arange(SPAN)[None, :]) % NPIX
        angle = 2.0 * np.pi * m / NPIX
        rows += [np.cos(angle), -np.sin(angle)]
    return np.concatenate(rows).astype(ml_dtypes.bfloat16)


def order_matrix():
    out = np.zeros((2 * KMAX, KMAX), np.float32)
    for place, rho in enumerate(ORDER):
        for kk in range(2):
            for t in range(N_TILE):
                j = 16 * t + 8 * kk + rho
                n = place * 64 + kk * N_TILE + t
                out[KMAX + j, n] = 1.0
                out[KMAX - j if j else 0, n] = 1.0
    return out.astype(ml_dtypes.bfloat16)


def edge_waves():
    step = lax.broadcasted_iota(jnp.int32, (1, SPAN), 1) & 7
    diag = jnp.where(step & 1 == 1, HALF, 1.0)
    cos = jnp.where(step & 3 == 2, 0.0, jnp.where((step >= 3) & (step <= 5), -diag, diag))
    sin = jnp.where(step & 3 == 0, 0.0, jnp.where(step >= 5, -diag, diag))
    return cos.astype(F32), sin.astype(F32)


def dft4(x, sign):
    (r0, i0), (r1, i1), (r2, i2), (r3, i3) = x
    ar, ai, br, bi = r0 + r2, i0 + i2, r0 - r2, i0 - i2
    cr, ci, dr, di = r1 + r3, i1 + i3, r1 - r3, i1 - i3
    if sign < 0:
        dr, di = -dr, -di
    return [(ar + cr, ai + ci), (br - di, bi + dr), (ar - cr, ai - ci), (br + di, bi - dr)]


def dft8(x, sign):
    even = dft4(x[0::2], sign)
    odd = dft4(x[1::2], sign)
    (r1, i1), (r2, i2), (r3, i3) = odd[1:]
    if sign > 0:
        turned = [odd[0], (HALF * (r1 - i1), HALF * (r1 + i1)), (-i2, r2), (-HALF * (r3 + i3), HALF * (r3 - i3))]
    else:
        turned = [odd[0], (HALF * (r1 + i1), HALF * (i1 - r1)), (i2, -r2), (HALF * (i3 - r3), -HALF * (r3 + i3))]
    low = [(a + c, b + d) for (a, b), (c, d) in zip(even, turned)]
    high = [(a - c, b - d) for (a, b), (c, d) in zip(even, turned)]
    return low + high


def dot_nt(a, b):
    return lax.dot_general(a, b, (((1,), (1,)), ((), ())), preferred_element_type=F32)


def dot_nn(a, b):
    return lax.dot_general(a, b, (((1,), (0,)), ((), ())), preferred_element_type=F32)


def dot_tn(a, b):
    return lax.dot_general(a, b, (((0,), (0,)), ((), ())), preferred_element_type=F32)


def table_of(table_ref, *rhos):
    start = PLACE[rhos[0]] * LANES
    return table_ref[start : start + LANES * len(rhos), :]


def columns_kernel(
    weight_ref, slab_ref, table_ref, out_ref, cells_ref, held_ref, fold_ref, band_ref,
    scale_ref, sems, table_sem, scale_sem,
):
    def fetch(chunk):
        rows = pl.ds(chunk * CHUNK, CHUNK)
        return pltpu.make_async_copy(slab_ref.at[0, :, rows, :], cells_ref.at[chunk], sems.at[chunk])

    def fetch_table():
        return pltpu.make_async_copy(table_ref, held_ref, table_sem)

    for chunk in range(CHUNKS):
        fetch(chunk).start(priority=chunk % 2)
    scales = pltpu.make_async_copy(weight_ref, scale_ref, scale_sem)
    scales.start()
    fetch_table().start()
    scales.wait()
    weights = [scale_ref[0, layer] for layer in range(slab_ref.shape[1])]

    def butterfly(chunk, start):
        def segment(m):
            cols = slice(m * SPAN + start, m * SPAN + start + LANES)
            total = cells_ref[chunk, 0, :, cols].astype(F32) * weights[0]
            for layer in range(1, len(weights)):
                total = total + cells_ref[chunk, layer, :, cols].astype(F32) * weights[layer]
            return total

        def keep(index, value):
            fold_ref[index, chunk * CHUNK : (chunk + 1) * CHUNK, start : start + LANES] = value.astype(BF16)

        x0, x4 = segment(0), segment(4)
        a0, a1 = x0 + x4, x0 - x4
        x2, x6 = segment(2), segment(6)
        a2, a3 = x2 + x6, x2 - x6
        x1, x5 = segment(1), segment(5)
        b0, b1 = x1 + x5, x1 - x5
        x3, x7 = segment(3), segment(7)
        b2, b3 = x3 + x7, x3 - x7
        total, other = a0 + a2, b0 + b2
        keep(0, total + other)
        keep(1, total - other)
        minus, plus = HALF * (b1 - b3), HALF * (b1 + b3)
        keep(2, a1 + minus)
        keep(3, -a3 - plus)
        keep(4, a0 - a2)
        keep(5, b2 - b0)
        keep(6, a1 - minus)
        keep(7, a3 - plus)

    for chunk in range(CHUNKS):
        fetch(chunk).wait()
        for start in range(0, SPAN, LANES):
            butterfly(chunk, start)
    fetch_table().wait()

    def place(rho, re, im):
        for s, part in enumerate((re, im)):
            for kk in range(2):
                start = 16 * s + 8 * kk + rho
                band_ref[pl.ds(start, N_TILE, stride=32), :] = part[kk * N_TILE : (kk + 1) * N_TILE]

    for rho in (0, 4):
        got = dot_nt(table_of(held_ref, rho), fold_ref[PLACE[rho]])
        place(rho, got[:64], got[64:])
    for number, (rho, back) in enumerate(DUOS):
        pair = fold_ref[2 + 2 * number : 4 + 2 * number].reshape(2 * ROWS, SPAN)
        got = dot_nt(table_of(held_ref, rho, back), pair)
        cu, cv = got[:64, :ROWS], got[:64, ROWS:]
        su, sv = got[64:128, :ROWS], got[64:128, ROWS:]
        place(rho, cu - sv, cv + su)
        cu, cv = got[128:192, :ROWS], got[128:192, ROWS:]
        su, sv = got[192:, :ROWS], got[192:, ROWS:]
        place(back, cu + sv, su - cv)
    out_ref[...] = band_ref[...].astype(BF16)


def columns(slab, weight, table):
    hbm = pl.BlockSpec(memory_space=pltpu.HBM)
    return pl.pallas_call(
        columns_kernel,
        in_specs=[hbm] * 3,
        out_specs=VMEM,
        out_shape=jax.ShapeDtypeStruct((2 * KMAX, ROWS), BF16),
        scratch_shapes=[
            pltpu.VMEM((CHUNKS, slab.shape[1], CHUNK, NPIX), BF16),
            pltpu.VMEM(table.shape, BF16),
            pltpu.VMEM((RADIX, ROWS, SPAN), BF16),
            pltpu.VMEM((2 * KMAX, ROWS), F32),
            pltpu.SMEM(weight.shape, F32),
            pltpu.SemaphoreType.DMA((CHUNKS,)),
            pltpu.SemaphoreType.DMA,
            pltpu.SemaphoreType.DMA,
        ],
        compiler_params=pltpu.CompilerParams(vmem_limit_bytes=60 * 1024 * 1024),
        name="columns",
    )(weight, slab, table)


def rows_kernel(band_ref, table_ref, ell_ref, out_ref, fold_ref):
    cos, sin = edge_waves()
    edge_re = jnp.zeros((16, 1), F32)
    edge_im = jnp.zeros((16, 1), F32)
    for u in range(SPAN // LANES):
        cols = slice(u * LANES, (u + 1) * LANES)
        starts = [(4 * m + u) * 32 for m in range(RADIX)]
        parts = [
            tuple(band_ref[start + 16 * s : start + 16 * s + 16, :].astype(F32) for s in range(2))
            for start in starts
        ]
        folded = dft8(parts, -1)
        for rho, (re, im) in enumerate(folded):
            fold_ref[PLACE[rho], 0:16, cols] = re.astype(BF16)
            fold_ref[PLACE[rho], 16:32, cols] = im.astype(BF16)
        up, vp = folded[0]
        edge_re = edge_re + jnp.sum(up * cos[:, cols] - vp * sin[:, cols], axis=1, keepdims=True)
        edge_im = edge_im + jnp.sum(vp * cos[:, cols] + up * sin[:, cols], axis=1, keepdims=True)
    lane = lax.broadcasted_iota(jnp.int32, (16, LANES), 1)
    low = lane < 64

    def lines(ahead, back):
        (cu, cv), (du, dv) = ahead, back
        real = jnp.where(low, cu - pltpu.roll(cv, 64, 1), pltpu.roll(du, 64, 1) + dv)
        imag = jnp.where(low, cv + pltpu.roll(cu, 64, 1), pltpu.roll(dv, 64, 1) - du)
        return real, imag

    def keep(rho, real, imag):
        cols = slice(PLACE[rho] * LANES, (PLACE[rho] + 1) * LANES)
        out_ref[0:16, cols] = real.astype(BF16)
        out_ref[16:32, cols] = imag.astype(BF16)

    for rho in (0, 4):
        got = dot_nt(fold_ref[PLACE[rho]], table_of(table_ref, rho))
        both = (got[:16], got[16:])
        real, imag = lines(both, both)
        if rho == 0:
            real = jnp.where(lane == 64, edge_re, real)
            imag = jnp.where(lane == 64, edge_im, imag)
        keep(rho, real, imag)
    for rho, back in DUOS:
        four = fold_ref[PLACE[rho] : PLACE[rho] + 2].reshape(64, SPAN)
        got = dot_nt(four, table_of(table_ref, rho, back))
        for place, one in enumerate((rho, back)):
            part = got[:, place * LANES : (place + 1) * LANES]
            duo = ((part[0:16], part[16:32]), (part[32:48], part[48:64]))
            keep(one, *lines(duo[place], duo[1 - place]))
    bins = ell_ref[...].astype(F32).astype(BF16)
    out_ref[0:16, 2 * KMAX :] = bins
    out_ref[16:32, 2 * KMAX :] = bins


def rows(band, table, ell):
    return pl.pallas_call(
        rows_kernel,
        in_specs=[VMEM, VMEM, VMEM],
        out_specs=VMEM,
        out_shape=jax.ShapeDtypeStruct((32, WIDTH), BF16),
        scratch_shapes=[pltpu.VMEM((RADIX, 32, SPAN), BF16)],
        compiler_params=pltpu.CompilerParams(vmem_limit_bytes=LIMIT),
        name="rows",
    )(band, table, ell)


def modes_kernel(
    index_ref, values_ref, *refs,
):
    (
        order_ref, kappa_ref, sums_ref, ell_ref, own_ref,
        lines_ref, terms_ref, picks_ref, entry_ref, value_ref,
    ) = refs[N_PLANE:]
    plane = lax.axis_index("plane")
    entry_ref[...] = jnp.zeros_like(entry_ref)
    entry_ref[0:BINS, 0:N_PLANE] = index_ref[...]
    value_ref[...] = jnp.zeros_like(value_ref)
    value_ref[:, 0 : values_ref.shape[1]] = jnp.broadcast_to(values_ref[...], (8, values_ref.shape[1]))
    kernel = jnp.take_along_axis(value_ref[...], entry_ref[...], axis=1)
    mine = jnp.where(lax.broadcasted_iota(jnp.int32, (8, LANES), 1) == plane, kernel, 0.0)
    own_ref[...] = jnp.broadcast_to(jnp.sum(mine, axis=1, keepdims=True), (8, LANES))
    for ref, bits in zip(refs, (0, 1, 2, 6, 4, 3, 7, 5)):
        lines_ref[plane ^ bits] = ref[...]
    bins = jnp.concatenate([lines_ref[p, 0:16, 2 * KMAX :] for p in range(N_PLANE)], axis=1)
    minus = dot_nn(bins[:, :KMAX], order_ref[:KMAX]).astype(jnp.int32)
    plus = dot_nn(bins[:, KMAX:], order_ref[KMAX:]).astype(jnp.int32)
    low = lax.broadcasted_iota(jnp.int32, (16, LANES), 1) < 64
    for pair in range(RADIX // 2):
        cols = slice(pair * LANES, (pair + 1) * LANES)
        ahead, back = plus[:, cols], minus[:, cols]
        ell_ref[:, 2 * pair * LANES : (2 * pair + 1) * LANES] = jnp.where(low, ahead, pltpu.roll(back, 64, 1))
        ell_ref[:, (2 * pair + 1) * LANES : (2 * pair + 2) * LANES] = jnp.where(low, pltpu.roll(ahead, 64, 1), back)
    weights = [
        [jnp.broadcast_to(kernel[b : b + 1, p : p + 1], (1, LANES)) for p in range(N_PLANE)] for b in range(BINS)
    ]
    for tile in range(RADIX):
        cols = slice(tile * LANES, (tile + 1) * LANES)
        kappa = [None] * BINS
        for p in range(N_PLANE):
            line = lines_ref[p, :, cols].astype(F32)
            for b in range(BINS):
                term = line * weights[b][p]
                kappa[b] = term if p == 0 else kappa[b] + term
        for b in range(BINS):
            kappa_ref[32 * b : 32 * b + 32, cols] = kappa[b]
        for number, (i, j) in enumerate(FIRST_GROUP + SECOND_GROUP):
            both = kappa[i] * kappa[j]
            term = both[0:16] + both[16:32]
            high = term.astype(BF16)
            terms_ref[16 * number : 16 * number + 16, cols] = high
            terms_ref[16 * (PAIRS + number) : 16 * (PAIRS + number) + 16, cols] = (
                term - high.astype(F32)
            ).astype(BF16)

    bin_row = lax.broadcasted_iota(jnp.int32, (16, 2 * KMAX), 0)
    for column in range(16):
        here = ell_ref[column : column + 1, :] == bin_row
        picks_ref[16 * column : 16 * column + 16, :] = jnp.where(here, 1.0, 0.0).astype(BF16)
    crossed = dot_nt(terms_ref[...], picks_ref[...])
    same = (lax.broadcasted_iota(jnp.int32, (16, 2 * LANES), 1) >> 4) == lax.broadcasted_iota(
        jnp.int32, (16, 2 * LANES), 0
    )
    lane = lax.broadcasted_iota(jnp.int32, (8, LANES), 1)
    sub = lax.broadcasted_iota(jnp.int32, (8, LANES), 0)
    spread = [jnp.zeros((8, LANES), F32), jnp.zeros((8, LANES), F32)]
    for number in range(PAIRS):
        low = 16 * (PAIRS + number)
        part = crossed[16 * number : 16 * number + 16] + crossed[low : low + 16]
        part = jnp.where(same, part, 0.0)
        part = part[0:8] + part[8:16]
        total = jnp.sum(part[:, :LANES] + part[:, LANES:], axis=0, keepdims=True)
        for shift in (64, 32, 16):
            total = total + pltpu.roll(total, shift, 1)
        group, row = divmod(number, 8)
        spread[group] = jnp.where(sub == row, total, spread[group])
    own = (lane >> 4) == sub
    sums = [jnp.sum(jnp.where(own, part, 0.0), axis=0, keepdims=True) for part in spread]
    pattern = jnp.where(sub & 1 == 0, sums[0], sums[1])
    sums_ref[...] = jnp.broadcast_to(pattern[None], (N_TILE // 4, 8, LANES)).reshape(2 * N_TILE, LANES)


def modes(index, values, group, order):
    return pl.pallas_call(
        modes_kernel,
        in_specs=[VMEM] * 11,
        out_specs=[VMEM] * 4,
        out_shape=[
            jax.ShapeDtypeStruct((32 * BINS, 2 * KMAX), F32),
            jax.ShapeDtypeStruct((2 * N_TILE, LANES), F32),
            jax.ShapeDtypeStruct((16, 2 * KMAX), jnp.int32),
            jax.ShapeDtypeStruct((8, LANES), F32),
        ],
        scratch_shapes=[
            pltpu.VMEM((N_PLANE, 32, WIDTH), BF16),
            pltpu.VMEM((2 * PAIRS * 16, 2 * KMAX), BF16),
            pltpu.VMEM((16 * ELLS, 2 * KMAX), BF16),
            pltpu.VMEM((8, LANES), jnp.int32),
            pltpu.VMEM((8, LANES), F32),
        ],
        compiler_params=pltpu.CompilerParams(vmem_limit_bytes=LIMIT),
        name="modes",
    )(index, values, *group, order)


def adjoint_kernel(
    own_ref, sums_ref, kappa_ref, ell_ref, target_ref, table_ref,
    spectra_ref, out_ref, weight_ref, line_ref, spread_ref,
):
    total = jnp.sum(sums_ref[...].reshape(N_TILE // 4, 8, LANES), axis=0)
    total = total + pltpu.roll(total, 2, 0)
    total = total + pltpu.roll(total, 4, 0)
    lane = lax.broadcasted_iota(jnp.int32, (1, LANES), 1)
    area = (2.0 * lane.astype(F32) + 1.0) * (float((KMAX // ELLS) ** 2) * (0.5 * math.pi))
    scale = float(NPIX * NPIX) * area
    for row, group in enumerate((FIRST_GROUP, SECOND_GROUP)):
        line = total[row : row + 1, :]
        for place, pair in enumerate(group):
            turned = line if place == 0 else pltpu.roll(line, LANES - 16 * place, 1)
            number = PAIR_ID[pair]
            spectra_ref[number : number + 1, :] = (turned / scale)[:, :ELLS]
    weight_ref[...] = jnp.zeros_like(weight_ref)
    weight_ref[0:10, 0:ELLS] = (spectra_ref[...] - target_ref[...]) * (
        float(KMAX) / (ELLS * NPIX)
    ) / area[:, :ELLS]

    couplings = []
    for number in range(PAIRS):
        row = weight_ref[number : number + 1, :]
        row = row + row if number in (PAIR_ID[(i, i)] for i in range(BINS)) else row
        couplings.append(jnp.broadcast_to(row, (8, LANES)))
    weights = [own_ref[b : b + 1, :] for b in range(BINS)]

    for tile in range(RADIX):
        cols = slice(tile * LANES, (tile + 1) * LANES)
        for half in range(0, 16, 8):
            where = ell_ref[half : half + 8, cols]
            mixers = [jnp.take_along_axis(table, where, axis=1) for table in couplings]
            for s in range(2):
                start = 16 * s + half
                kappa = [kappa_ref[32 * b + start : 32 * b + start + 8, cols] for b in range(BINS)]
                line = None
                for i in range(BINS):
                    grad = mixers[PAIR_ID[(i, 0)]] * kappa[0]
                    for j in range(1, BINS):
                        grad = grad + mixers[PAIR_ID[(i, j)]] * kappa[j]
                    term = grad.astype(BF16).astype(F32) * weights[i]
                    line = term if i == 0 else line + term
                line_ref[start : start + 8, cols] = line

    wide_lane = lax.broadcasted_iota(jnp.int32, (16, LANES), 1)
    low = wide_lane < 64

    def factors(rho):
        cols = slice(PLACE[rho] * LANES, (PLACE[rho] + 1) * LANES)
        g0, g1 = line_ref[0:16, cols], line_ref[16:32, cols]
        if rho == 0:
            g0 = jnp.where(wide_lane == 64, 0.0, g0)
            g1 = jnp.where(wide_lane == 64, 0.0, g1)
        t0, t1 = pltpu.roll(g0, 64, 1), pltpu.roll(g1, 64, 1)
        ahead = (jnp.where(low, g0, t1), jnp.where(low, g1, -t0))
        back = (jnp.where(low, t0, -g1), jnp.where(low, t1, g0))
        return ahead, back

    def spread(rho, re, im):
        spread_ref[2 * rho] = re
        spread_ref[2 * rho + 1] = im

    start = PLACE[0] * LANES + 64
    edge0 = line_ref[0:16, start : start + 1]
    edge1 = line_ref[16:32, start : start + 1]
    cos, sin = edge_waves()
    for rho in (0, 4):
        ahead, back = factors(rho)
        left = jnp.concatenate([ahead[0] + back[0], ahead[1] + back[1]], axis=0).astype(BF16)
        got = dot_nn(left, table_of(table_ref, rho))
        re, im = got[:16], got[16:]
        if rho == 0:
            re = re + edge0 * cos + edge1 * sin
            im = im + edge1 * cos - edge0 * sin
        spread(rho, re, im)
    for rho, back in DUOS:
        plus, minus = factors(rho)
        plus_back, minus_back = factors(back)
        left = jnp.concatenate(
            [
                jnp.concatenate(plus + minus, axis=0),
                jnp.concatenate(minus_back + plus_back, axis=0),
            ],
            axis=1,
        ).astype(BF16)
        got = dot_nn(left, table_of(table_ref, rho, back))
        spread(rho, got[0:16], got[16:32])
        spread(back, got[32:48], got[48:64])
    for u in range(SPAN // LANES):
        cols = slice(u * LANES, (u + 1) * LANES)
        parts = [(spread_ref[2 * rho, :, cols], spread_ref[2 * rho + 1, :, cols]) for rho in range(RADIX)]
        for m, both in enumerate(dft8(parts, 1)):
            for s in range(2):
                begin = (4 * m + u) * 32 + 16 * s
                out_ref[begin : begin + 16, :] = both[s].astype(BF16)


def adjoint(own, sums, kappa, ell, target, table):
    return pl.pallas_call(
        adjoint_kernel,
        in_specs=[VMEM] * 6,
        out_specs=[VMEM, VMEM],
        out_shape=[
            jax.ShapeDtypeStruct(target.shape, F32),
            jax.ShapeDtypeStruct((2 * KMAX, ROWS), BF16),
        ],
        scratch_shapes=[
            pltpu.VMEM((16, LANES), F32),
            pltpu.VMEM((32, 2 * KMAX), F32),
            pltpu.VMEM((2 * RADIX, 16, SPAN), F32),
        ],
        compiler_params=pltpu.CompilerParams(vmem_limit_bytes=LIMIT),
        name="adjoint",
    )(own, sums, kappa, ell, target, table)


def maps_kernel(band_ref, table_ref, out_ref, wide_ref, spread_ref, done_ref, sems):
    wide_ref[...] = band_ref[...].astype(F32)

    def block(rho, s):
        parts = [
            wide_ref[pl.ds(16 * s + 8 * kk + rho, N_TILE, stride=32), :] for kk in range(2)
        ]
        return jnp.concatenate(parts, axis=0)

    flat = []
    for rho in (0, 4):
        left = jnp.concatenate([block(rho, 0), block(rho, 1)], axis=0).astype(BF16)
        flat.append(dot_tn(left, table_of(table_ref, rho)))
    p, q = [None], [None]
    for rho, back in DUOS:
        b0, b1, e0, e1 = block(rho, 0), block(rho, 1), block(back, 0), block(back, 1)
        left = jnp.concatenate(
            [
                jnp.concatenate([b0, b1, e0, e1], axis=0),
                jnp.concatenate([b1, -b0, -e1, e0], axis=0),
            ],
            axis=1,
        ).astype(BF16)
        got = dot_tn(left, table_of(table_ref, rho, back))
        p.append(got[:ROWS])
        q.append(got[ROWS:])
    for index, part in enumerate(flat + p[1:] + q[1:]):
        spread_ref[index] = part

    def send(chunk):
        rows = pl.ds(chunk * CHUNK, CHUNK)
        return pltpu.make_async_copy(done_ref.at[rows, :], out_ref.at[0, rows, :], sems.at[chunk])

    for chunk in range(CHUNKS):
        rows = slice(chunk * CHUNK, (chunk + 1) * CHUNK)
        for start in range(0, SPAN, LANES):
            cols = slice(start, start + LANES)
            a0, a4, p1, p2, p3, q1, q2, q3 = (spread_ref[index, rows, cols] for index in range(RADIX))

            def put(m, even, odd):
                done_ref[rows, m * SPAN + start : m * SPAN + start + LANES] = even + odd
                done_ref[rows, (m + 4) * SPAN + start : (m + 4) * SPAN + start + LANES] = even - odd

            plus, minus = a0 + a4, a0 - a4
            put(0, plus + p2, p1 + p3)
            put(1, minus - q2, HALF * (p1 - q1 - p3 - q3))
            put(2, plus - p2, q3 - q1)
            put(3, minus + q2, HALF * (p3 - p1 - q1 - q3))
        send(chunk).start()
    for chunk in range(CHUNKS):
        send(chunk).wait()


def maps(band, table):
    return pl.pallas_call(
        maps_kernel,
        in_specs=[VMEM, VMEM],
        out_specs=pl.BlockSpec(memory_space=pltpu.HBM),
        out_shape=jax.ShapeDtypeStruct((1, ROWS, NPIX), F32),
        scratch_shapes=[
            pltpu.VMEM((2 * KMAX, ROWS), F32),
            pltpu.VMEM((RADIX, ROWS, SPAN), F32),
            pltpu.VMEM((ROWS, NPIX), F32),
            pltpu.SemaphoreType.DMA((CHUNKS,)),
        ],
        compiler_params=pltpu.CompilerParams(vmem_limit_bytes=LIMIT),
        name="maps",
    )(band, table)


def body(slab_cells, slab_weight, kernel_table, kernel_index, ell_index, target_spectra):
    table = jnp.asarray(wave_table())
    order = jnp.asarray(order_matrix())
    exchange = functools.partial(
        lax.all_to_all, axis_name="tile", split_axis=0, concat_axis=0, tiled=True
    )

    def swap(value, bits):
        return lax.ppermute(value, "plane", [(p, p ^ bits) for p in range(N_PLANE)])

    band = exchange(columns(slab_cells, slab_weight, table))
    lines = rows(band, table, ell_index.T)
    across = swap(lines, 1)
    group = [lines, across]
    for part in (lines, across):
        group += [swap(part, bits) for bits in (2, 6, 4)]
    kappa, sums, ell, own = modes(kernel_index, kernel_table.reshape(1, -1), group, order)
    spectra, adjoint_band = adjoint(
        own, exchange(sums), kappa, ell, target_spectra, table
    )
    return spectra, maps(exchange(adjoint_band), table)


def solution(mesh):
    return jax.shard_map(
        body,
        mesh=mesh,
        in_specs=(
            P("plane", None, "tile", None),
            P("plane", None),
            P(),
            P(),
            P("plane", "tile"),
            P(),
        ),
        out_specs=(P(), P("plane", "tile", None)),
        check_vma=False,
    )
```

```python
import functools
import math

import jax
import jax.numpy as jnp
import ml_dtypes
import numpy as np
from jax import lax
from jax.experimental import pallas as pl
from jax.experimental.pallas import tpu as pltpu
from jax.sharding import PartitionSpec as P

NPIX = 4096
KMAX = 512
BINS = 4
ELLS = 16
RADIX = 8
SPAN = NPIX // RADIX
N_PLANE = 8
N_TILE = 32
ROWS = NPIX // N_TILE
LANES = 128
CHUNK = 16
WIDTH = 2 * KMAX + ROWS
PAIRS = BINS * (BINS + 1) // 2
CHUNKS = ROWS // CHUNK
STRIP = 32
STRIPS = ROWS // STRIP

ORDER = (0, 4, 1, 7, 2, 6, 3, 5)
PLACE = {rho: place for place, rho in enumerate(ORDER)}
DUOS = ((1, 7), (2, 6), (3, 5))
HALF = math.sqrt(0.5)

PAIR_ID = {}
for _number, (_i, _j) in enumerate(zip(*np.triu_indices(BINS))):
    PAIR_ID[(int(_i), int(_j))] = PAIR_ID[(int(_j), int(_i))] = _number
FIRST_GROUP = ((0, 0), (1, 1), (2, 2), (3, 3), (0, 1), (1, 2), (2, 3), (3, 0))
SECOND_GROUP = ((0, 2), (1, 3))

F32 = jnp.float32
BF16 = jnp.bfloat16
VMEM = pl.BlockSpec(memory_space=pltpu.VMEM)
SMEM = pl.BlockSpec(memory_space=pltpu.SMEM)
LIMIT = 32 * 1024 * 1024


def wave_table():
    rows = []
    tiles = np.arange(N_TILE)
    for rho in ORDER:
        k = np.concatenate([16 * tiles + 8 * kk + rho for kk in range(2)])
        m = (k[:, None] * np.arange(SPAN)[None, :]) % NPIX
        angle = 2.0 * np.pi * m / NPIX
        rows += [np.cos(angle), -np.sin(angle)]
    return np.concatenate(rows).astype(ml_dtypes.bfloat16)


def order_matrix():
    out = np.zeros((2 * KMAX, KMAX), np.float32)
    for place, rho in enumerate(ORDER):
        for kk in range(2):
            for t in range(N_TILE):
                j = 16 * t + 8 * kk + rho
                n = place * 64 + kk * N_TILE + t
                out[KMAX + j, n] = 1.0
                out[KMAX - j if j else 0, n] = 1.0
    return out.astype(ml_dtypes.bfloat16)


def edge_waves():
    step = lax.broadcasted_iota(jnp.int32, (1, SPAN), 1) & 7
    diag = jnp.where(step & 1 == 1, HALF, 1.0)
    cos = jnp.where(step & 3 == 2, 0.0, jnp.where((step >= 3) & (step <= 5), -diag, diag))
    sin = jnp.where(step & 3 == 0, 0.0, jnp.where(step >= 5, -diag, diag))
    return cos.astype(F32), sin.astype(F32)


def dft4(x, sign):
    (r0, i0), (r1, i1), (r2, i2), (r3, i3) = x
    ar, ai, br, bi = r0 + r2, i0 + i2, r0 - r2, i0 - i2
    cr, ci, dr, di = r1 + r3, i1 + i3, r1 - r3, i1 - i3
    if sign < 0:
        dr, di = -dr, -di
    return [(ar + cr, ai + ci), (br - di, bi + dr), (ar - cr, ai - ci), (br + di, bi - dr)]


def dft8(x, sign):
    even = dft4(x[0::2], sign)
    odd = dft4(x[1::2], sign)
    (r1, i1), (r2, i2), (r3, i3) = odd[1:]
    if sign > 0:
        turned = [odd[0], (HALF * (r1 - i1), HALF * (r1 + i1)), (-i2, r2), (-HALF * (r3 + i3), HALF * (r3 - i3))]
    else:
        turned = [odd[0], (HALF * (r1 + i1), HALF * (i1 - r1)), (i2, -r2), (HALF * (i3 - r3), -HALF * (r3 + i3))]
    low = [(a + c, b + d) for (a, b), (c, d) in zip(even, turned)]
    high = [(a - c, b - d) for (a, b), (c, d) in zip(even, turned)]
    return low + high


def dot_nt(a, b):
    return lax.dot_general(a, b, (((1,), (1,)), ((), ())), preferred_element_type=F32)


def dot_nn(a, b):
    return lax.dot_general(a, b, (((1,), (0,)), ((), ())), preferred_element_type=F32)


def dot_tn(a, b):
    return lax.dot_general(a, b, (((0,), (0,)), ((), ())), preferred_element_type=F32)


def table_of(table_ref, *rhos):
    start = PLACE[rhos[0]] * LANES
    return table_ref[start : start + LANES * len(rhos), :]


def columns_kernel(
    weight_ref, slab_ref, table_ref, out_ref, cells_ref, held_ref, fold_ref, band_ref,
    scale_ref, sems, table_sem, scale_sem,
):
    def fetch(chunk):
        rows = pl.ds(chunk * CHUNK, CHUNK)
        return pltpu.make_async_copy(slab_ref.at[0, :, rows, :], cells_ref.at[chunk], sems.at[chunk])

    def fetch_table():
        return pltpu.make_async_copy(table_ref, held_ref, table_sem)

    for chunk in range(CHUNKS):
        fetch(chunk).start(priority=chunk % 2)
    scales = pltpu.make_async_copy(weight_ref, scale_ref, scale_sem)
    scales.start()
    fetch_table().start()
    scales.wait()
    weights = [scale_ref[0, layer] for layer in range(slab_ref.shape[1])]

    def butterfly(chunk, start):
        def segment(m):
            cols = slice(m * SPAN + start, m * SPAN + start + LANES)
            total = cells_ref[chunk, 0, :, cols].astype(F32) * weights[0]
            for layer in range(1, len(weights)):
                total = total + cells_ref[chunk, layer, :, cols].astype(F32) * weights[layer]
            return total

        def keep(index, value):
            fold_ref[index, chunk * CHUNK : (chunk + 1) * CHUNK, start : start + LANES] = value.astype(BF16)

        x0, x4 = segment(0), segment(4)
        a0, a1 = x0 + x4, x0 - x4
        x2, x6 = segment(2), segment(6)
        a2, a3 = x2 + x6, x2 - x6
        x1, x5 = segment(1), segment(5)
        b0, b1 = x1 + x5, x1 - x5
        x3, x7 = segment(3), segment(7)
        b2, b3 = x3 + x7, x3 - x7
        total, other = a0 + a2, b0 + b2
        keep(0, total + other)
        keep(1, total - other)
        minus, plus = HALF * (b1 - b3), HALF * (b1 + b3)
        keep(2, a1 + minus)
        keep(3, -a3 - plus)
        keep(4, a0 - a2)
        keep(5, b2 - b0)
        keep(6, a1 - minus)
        keep(7, a3 - plus)

    for chunk in range(CHUNKS):
        fetch(chunk).wait()
        for start in range(0, SPAN, LANES):
            butterfly(chunk, start)
    fetch_table().wait()

    def place(rho, re, im):
        for s, part in enumerate((re, im)):
            for kk in range(2):
                start = 16 * s + 8 * kk + rho
                band_ref[pl.ds(start, N_TILE, stride=32), :] = part[kk * N_TILE : (kk + 1) * N_TILE]

    for rho in (0, 4):
        got = dot_nt(table_of(held_ref, rho), fold_ref[PLACE[rho]])
        place(rho, got[:64], got[64:])
    for number, (rho, back) in enumerate(DUOS):
        pair = fold_ref[2 + 2 * number : 4 + 2 * number].reshape(2 * ROWS, SPAN)
        got = dot_nt(table_of(held_ref, rho, back), pair)
        cu, cv = got[:64, :ROWS], got[:64, ROWS:]
        su, sv = got[64:128, :ROWS], got[64:128, ROWS:]
        place(rho, cu - sv, cv + su)
        cu, cv = got[128:192, :ROWS], got[128:192, ROWS:]
        su, sv = got[192:, :ROWS], got[192:, ROWS:]
        place(back, cu + sv, su - cv)
    out_ref[...] = band_ref[...].astype(BF16)


def columns(slab, weight, table):
    hbm = pl.BlockSpec(memory_space=pltpu.HBM)
    return pl.pallas_call(
        columns_kernel,
        in_specs=[hbm] * 3,
        out_specs=VMEM,
        out_shape=jax.ShapeDtypeStruct((2 * KMAX, ROWS), BF16),
        scratch_shapes=[
            pltpu.VMEM((CHUNKS, slab.shape[1], CHUNK, NPIX), BF16),
            pltpu.VMEM(table.shape, BF16),
            pltpu.VMEM((RADIX, ROWS, SPAN), BF16),
            pltpu.VMEM((2 * KMAX, ROWS), F32),
            pltpu.SMEM(weight.shape, F32),
            pltpu.SemaphoreType.DMA((CHUNKS,)),
            pltpu.SemaphoreType.DMA,
            pltpu.SemaphoreType.DMA,
        ],
        compiler_params=pltpu.CompilerParams(vmem_limit_bytes=60 * 1024 * 1024),
        name="columns",
    )(weight, slab, table)


def rows_kernel(band_ref, table_ref, ell_ref, out_ref, fold_ref):
    cos, sin = edge_waves()
    edge_re = jnp.zeros((16, 1), F32)
    edge_im = jnp.zeros((16, 1), F32)
    for u in range(SPAN // LANES):
        cols = slice(u * LANES, (u + 1) * LANES)
        starts = [(4 * m + u) * 32 for m in range(RADIX)]
        parts = [
            tuple(band_ref[start + 16 * s : start + 16 * s + 16, :].astype(F32) for s in range(2))
            for start in starts
        ]
        folded = dft8(parts, -1)
        for rho, (re, im) in enumerate(folded):
            fold_ref[PLACE[rho], 0:16, cols] = re.astype(BF16)
            fold_ref[PLACE[rho], 16:32, cols] = im.astype(BF16)
        up, vp = folded[0]
        edge_re = edge_re + jnp.sum(up * cos[:, cols] - vp * sin[:, cols], axis=1, keepdims=True)
        edge_im = edge_im + jnp.sum(vp * cos[:, cols] + up * sin[:, cols], axis=1, keepdims=True)
    lane = lax.broadcasted_iota(jnp.int32, (16, LANES), 1)
    low = lane < 64

    def lines(ahead, back):
        (cu, cv), (du, dv) = ahead, back
        real = jnp.where(low, cu - pltpu.roll(cv, 64, 1), pltpu.roll(du, 64, 1) + dv)
        imag = jnp.where(low, cv + pltpu.roll(cu, 64, 1), pltpu.roll(dv, 64, 1) - du)
        return real, imag

    def keep(rho, real, imag):
        cols = slice(PLACE[rho] * LANES, (PLACE[rho] + 1) * LANES)
        out_ref[0:16, cols] = real.astype(BF16)
        out_ref[16:32, cols] = imag.astype(BF16)

    for rho in (0, 4):
        got = dot_nt(fold_ref[PLACE[rho]], table_of(table_ref, rho))
        both = (got[:16], got[16:])
        real, imag = lines(both, both)
        if rho == 0:
            real = jnp.where(lane == 64, edge_re, real)
            imag = jnp.where(lane == 64, edge_im, imag)
        keep(rho, real, imag)
    for rho, back in DUOS:
        four = fold_ref[PLACE[rho] : PLACE[rho] + 2].reshape(64, SPAN)
        got = dot_nt(four, table_of(table_ref, rho, back))
        for place, one in enumerate((rho, back)):
            part = got[:, place * LANES : (place + 1) * LANES]
            duo = ((part[0:16], part[16:32]), (part[32:48], part[48:64]))
            keep(one, *lines(duo[place], duo[1 - place]))
    bins = ell_ref[...].astype(F32).astype(BF16)
    out_ref[0:16, 2 * KMAX :] = bins
    out_ref[16:32, 2 * KMAX :] = bins


def rows(band, table, ell):
    return pl.pallas_call(
        rows_kernel,
        in_specs=[VMEM, VMEM, VMEM],
        out_specs=VMEM,
        out_shape=jax.ShapeDtypeStruct((32, WIDTH), BF16),
        scratch_shapes=[pltpu.VMEM((RADIX, 32, SPAN), BF16)],
        compiler_params=pltpu.CompilerParams(vmem_limit_bytes=LIMIT),
        name="rows",
    )(band, table, ell)


def modes_kernel(
    index_ref, values_ref, *refs,
):
    (
        order_ref, kappa_ref, sums_ref, ell_ref, own_ref,
        lines_ref, terms_ref, picks_ref, entry_ref, value_ref,
    ) = refs[N_PLANE:]
    plane = lax.axis_index("plane")
    entry_ref[...] = jnp.zeros_like(entry_ref)
    entry_ref[0:BINS, 0:N_PLANE] = index_ref[...]
    value_ref[...] = jnp.zeros_like(value_ref)
    value_ref[:, 0 : values_ref.shape[1]] = jnp.broadcast_to(values_ref[...], (8, values_ref.shape[1]))
    kernel = jnp.take_along_axis(value_ref[...], entry_ref[...], axis=1)
    mine = jnp.where(lax.broadcasted_iota(jnp.int32, (8, LANES), 1) == plane, kernel, 0.0)
    own_ref[...] = jnp.broadcast_to(jnp.sum(mine, axis=1, keepdims=True), (8, LANES))
    for ref, bits in zip(refs, (0, 1, 2, 6, 4, 3, 7, 5)):
        lines_ref[plane ^ bits] = ref[...]
    bins = jnp.concatenate([lines_ref[p, 0:16, 2 * KMAX :] for p in range(N_PLANE)], axis=1)
    minus = dot_nn(bins[:, :KMAX], order_ref[:KMAX]).astype(jnp.int32)
    plus = dot_nn(bins[:, KMAX:], order_ref[KMAX:]).astype(jnp.int32)
    low = lax.broadcasted_iota(jnp.int32, (16, LANES), 1) < 64
    for pair in range(RADIX // 2):
        cols = slice(pair * LANES, (pair + 1) * LANES)
        ahead, back = plus[:, cols], minus[:, cols]
        ell_ref[:, 2 * pair * LANES : (2 * pair + 1) * LANES] = jnp.where(low, ahead, pltpu.roll(back, 64, 1))
        ell_ref[:, (2 * pair + 1) * LANES : (2 * pair + 2) * LANES] = jnp.where(low, pltpu.roll(ahead, 64, 1), back)
    weights = [
        [jnp.broadcast_to(kernel[b : b + 1, p : p + 1], (1, LANES)) for p in range(N_PLANE)] for b in range(BINS)
    ]
    for tile in range(RADIX):
        cols = slice(tile * LANES, (tile + 1) * LANES)
        kappa = [None] * BINS
        for p in range(N_PLANE):
            line = lines_ref[p, :, cols].astype(F32)
            for b in range(BINS):
                term = line * weights[b][p]
                kappa[b] = term if p == 0 else kappa[b] + term
        for b in range(BINS):
            kappa_ref[32 * b : 32 * b + 32, cols] = kappa[b]
        for number, (i, j) in enumerate(FIRST_GROUP + SECOND_GROUP):
            both = kappa[i] * kappa[j]
            term = both[0:16] + both[16:32]
            high = term.astype(BF16)
            terms_ref[16 * number : 16 * number + 16, cols] = high
            terms_ref[16 * (PAIRS + number) : 16 * (PAIRS + number) + 16, cols] = (
                term - high.astype(F32)
            ).astype(BF16)

    bin_row = lax.broadcasted_iota(jnp.int32, (16, 2 * KMAX), 0)
    for column in range(16):
        here = ell_ref[column : column + 1, :] == bin_row
        picks_ref[16 * column : 16 * column + 16, :] = jnp.where(here, 1.0, 0.0).astype(BF16)
    crossed = dot_nt(terms_ref[...], picks_ref[...])
    same = (lax.broadcasted_iota(jnp.int32, (16, 2 * LANES), 1) >> 4) == lax.broadcasted_iota(
        jnp.int32, (16, 2 * LANES), 0
    )
    lane = lax.broadcasted_iota(jnp.int32, (8, LANES), 1)
    sub = lax.broadcasted_iota(jnp.int32, (8, LANES), 0)
    spread = [jnp.zeros((8, LANES), F32), jnp.zeros((8, LANES), F32)]
    for number in range(PAIRS):
        low = 16 * (PAIRS + number)
        part = crossed[16 * number : 16 * number + 16] + crossed[low : low + 16]
        part = jnp.where(same, part, 0.0)
        part = part[0:8] + part[8:16]
        total = jnp.sum(part[:, :LANES] + part[:, LANES:], axis=0, keepdims=True)
        for shift in (64, 32, 16):
            total = total + pltpu.roll(total, shift, 1)
        group, row = divmod(number, 8)
        spread[group] = jnp.where(sub == row, total, spread[group])
    own = (lane >> 4) == sub
    sums = [jnp.sum(jnp.where(own, part, 0.0), axis=0, keepdims=True) for part in spread]
    pattern = jnp.where(sub & 1 == 0, sums[0], sums[1])
    sums_ref[...] = jnp.broadcast_to(pattern[None], (N_TILE // 4, 8, LANES)).reshape(2 * N_TILE, LANES)


def modes(index, values, group, order):
    return pl.pallas_call(
        modes_kernel,
        in_specs=[VMEM] * 11,
        out_specs=[VMEM] * 4,
        out_shape=[
            jax.ShapeDtypeStruct((32 * BINS, 2 * KMAX), F32),
            jax.ShapeDtypeStruct((2 * N_TILE, LANES), F32),
            jax.ShapeDtypeStruct((16, 2 * KMAX), jnp.int32),
            jax.ShapeDtypeStruct((8, LANES), F32),
        ],
        scratch_shapes=[
            pltpu.VMEM((N_PLANE, 32, WIDTH), BF16),
            pltpu.VMEM((2 * PAIRS * 16, 2 * KMAX), BF16),
            pltpu.VMEM((16 * ELLS, 2 * KMAX), BF16),
            pltpu.VMEM((8, LANES), jnp.int32),
            pltpu.VMEM((8, LANES), F32),
        ],
        compiler_params=pltpu.CompilerParams(vmem_limit_bytes=LIMIT),
        name="modes",
    )(index, values, *group, order)


def adjoint_kernel(
    own_ref, sums_ref, kappa_ref, ell_ref, target_ref, table_ref,
    spectra_ref, out_ref, weight_ref, line_ref, spread_ref,
):
    total = jnp.sum(sums_ref[...].reshape(N_TILE // 4, 8, LANES), axis=0)
    total = total + pltpu.roll(total, 2, 0)
    total = total + pltpu.roll(total, 4, 0)
    lane = lax.broadcasted_iota(jnp.int32, (1, LANES), 1)
    area = (2.0 * lane.astype(F32) + 1.0) * (float((KMAX // ELLS) ** 2) * (0.5 * math.pi))
    scale = float(NPIX * NPIX) * area
    for row, group in enumerate((FIRST_GROUP, SECOND_GROUP)):
        line = total[row : row + 1, :]
        for place, pair in enumerate(group):
            turned = line if place == 0 else pltpu.roll(line, LANES - 16 * place, 1)
            number = PAIR_ID[pair]
            spectra_ref[number : number + 1, :] = (turned / scale)[:, :ELLS]
    weight_ref[...] = jnp.zeros_like(weight_ref)
    weight_ref[0:10, 0:ELLS] = (spectra_ref[...] - target_ref[...]) * (
        float(KMAX) / (ELLS * NPIX)
    ) / area[:, :ELLS]

    tables = []
    for j in range(BINS):
        total = None
        for i in range(BINS):
            number = PAIR_ID[(i, j)]
            row = weight_ref[number : number + 1, :]
            term = own_ref[i : i + 1, :] * (row + row if i == j else row)
            total = term if total is None else total + term
        tables.append(jnp.broadcast_to(total, (8, LANES)))

    for tile in range(RADIX):
        cols = slice(tile * LANES, (tile + 1) * LANES)
        for half in range(0, 16, 8):
            where = ell_ref[half : half + 8, cols]
            mixers = [jnp.take_along_axis(table, where, axis=1) for table in tables]
            for s in range(2):
                start = 16 * s + half
                line = mixers[0] * kappa_ref[start : start + 8, cols]
                for j in range(1, BINS):
                    line = line + mixers[j] * kappa_ref[32 * j + start : 32 * j + start + 8, cols]
                line_ref[start : start + 8, cols] = line

    wide_lane = lax.broadcasted_iota(jnp.int32, (16, LANES), 1)
    low = wide_lane < 64

    def factors(rho):
        cols = slice(PLACE[rho] * LANES, (PLACE[rho] + 1) * LANES)
        g0, g1 = line_ref[0:16, cols], line_ref[16:32, cols]
        if rho == 0:
            g0 = jnp.where(wide_lane == 64, 0.0, g0)
            g1 = jnp.where(wide_lane == 64, 0.0, g1)
        t0, t1 = pltpu.roll(g0, 64, 1), pltpu.roll(g1, 64, 1)
        ahead = (jnp.where(low, g0, t1), jnp.where(low, g1, -t0))
        back = (jnp.where(low, t0, -g1), jnp.where(low, t1, g0))
        return ahead, back

    def spread(rho, re, im):
        spread_ref[2 * rho] = re
        spread_ref[2 * rho + 1] = im

    start = PLACE[0] * LANES + 64
    edge0 = line_ref[0:16, start : start + 1]
    edge1 = line_ref[16:32, start : start + 1]
    cos, sin = edge_waves()
    for rho in (0, 4):
        ahead, back = factors(rho)
        left = jnp.concatenate([ahead[0] + back[0], ahead[1] + back[1]], axis=0).astype(BF16)
        got = dot_nn(left, table_of(table_ref, rho))
        re, im = got[:16], got[16:]
        if rho == 0:
            re = re + edge0 * cos + edge1 * sin
            im = im + edge1 * cos - edge0 * sin
        spread(rho, re, im)
    for rho, back in DUOS:
        plus, minus = factors(rho)
        plus_back, minus_back = factors(back)
        left = jnp.concatenate(
            [
                jnp.concatenate(plus + minus, axis=0),
                jnp.concatenate(minus_back + plus_back, axis=0),
            ],
            axis=1,
        ).astype(BF16)
        got = dot_nn(left, table_of(table_ref, rho, back))
        spread(rho, got[0:16], got[16:32])
        spread(back, got[32:48], got[48:64])
    for u in range(SPAN // LANES):
        cols = slice(u * LANES, (u + 1) * LANES)
        parts = [(spread_ref[2 * rho, :, cols], spread_ref[2 * rho + 1, :, cols]) for rho in range(RADIX)]
        for m, both in enumerate(dft8(parts, 1)):
            for s in range(2):
                begin = (4 * m + u) * 32 + 16 * s
                out_ref[begin : begin + 16, :] = both[s].astype(BF16)


def adjoint(own, sums, kappa, ell, target, table):
    return pl.pallas_call(
        adjoint_kernel,
        in_specs=[VMEM] * 6,
        out_specs=[VMEM, VMEM],
        out_shape=[
            jax.ShapeDtypeStruct(target.shape, F32),
            jax.ShapeDtypeStruct((2 * KMAX, ROWS), BF16),
        ],
        scratch_shapes=[
            pltpu.VMEM((16, LANES), F32),
            pltpu.VMEM((32, 2 * KMAX), F32),
            pltpu.VMEM((2 * RADIX, 16, SPAN), F32),
        ],
        compiler_params=pltpu.CompilerParams(vmem_limit_bytes=LIMIT),
        name="adjoint",
    )(own, sums, kappa, ell, target, table)


def maps_kernel(band_ref, table_ref, out_ref, wide_ref, spread_ref, done_ref, sems):
    wide_ref[...] = band_ref[...].astype(F32)

    def block(rho, s):
        parts = [
            wide_ref[pl.ds(16 * s + 8 * kk + rho, N_TILE, stride=32), :] for kk in range(2)
        ]
        return jnp.concatenate(parts, axis=0)

    flat = []
    for rho in (0, 4):
        left = jnp.concatenate([block(rho, 0), block(rho, 1)], axis=0).astype(BF16)
        flat.append(dot_tn(left, table_of(table_ref, rho)))
    p, q = [None], [None]
    for rho, back in DUOS:
        b0, b1, e0, e1 = block(rho, 0), block(rho, 1), block(back, 0), block(back, 1)
        left = jnp.concatenate(
            [
                jnp.concatenate([b0, b1, e0, e1], axis=0),
                jnp.concatenate([b1, -b0, -e1, e0], axis=0),
            ],
            axis=1,
        ).astype(BF16)
        got = dot_tn(left, table_of(table_ref, rho, back))
        p.append(got[:ROWS])
        q.append(got[ROWS:])
    for index, part in enumerate(flat + p[1:] + q[1:]):
        spread_ref[index] = part

    def send(chunk):
        rows = pl.ds(chunk * STRIP, STRIP)
        return pltpu.make_async_copy(done_ref.at[rows, :], out_ref.at[0, rows, :], sems.at[chunk])

    for chunk in range(STRIPS):
        rows = slice(chunk * STRIP, (chunk + 1) * STRIP)
        for start in range(0, SPAN, LANES):
            cols = slice(start, start + LANES)
            a0, a4, p1, p2, p3, q1, q2, q3 = (spread_ref[index, rows, cols] for index in range(RADIX))

            def put(m, even, odd):
                done_ref[rows, m * SPAN + start : m * SPAN + start + LANES] = even + odd
                done_ref[rows, (m + 4) * SPAN + start : (m + 4) * SPAN + start + LANES] = even - odd

            plus, minus = a0 + a4, a0 - a4
            put(0, plus + p2, p1 + p3)
            put(1, minus - q2, HALF * (p1 - q1 - p3 - q3))
            put(2, plus - p2, q3 - q1)
            put(3, minus + q2, HALF * (p3 - p1 - q1 - q3))
        send(chunk).start()
    for chunk in range(STRIPS):
        send(chunk).wait()


def maps(band, table):
    return pl.pallas_call(
        maps_kernel,
        in_specs=[VMEM, VMEM],
        out_specs=pl.BlockSpec(memory_space=pltpu.HBM),
        out_shape=jax.ShapeDtypeStruct((1, ROWS, NPIX), F32),
        scratch_shapes=[
            pltpu.VMEM((2 * KMAX, ROWS), F32),
            pltpu.VMEM((RADIX, ROWS, SPAN), F32),
            pltpu.VMEM((ROWS, NPIX), F32),
            pltpu.SemaphoreType.DMA((STRIPS,)),
        ],
        compiler_params=pltpu.CompilerParams(vmem_limit_bytes=LIMIT),
        name="maps",
    )(band, table)


def body(slab_cells, slab_weight, kernel_table, kernel_index, ell_index, target_spectra):
    table = jnp.asarray(wave_table())
    order = jnp.asarray(order_matrix())
    exchange = functools.partial(
        lax.all_to_all, axis_name="tile", split_axis=0, concat_axis=0, tiled=True
    )

    def swap(value, bits):
        return lax.ppermute(value, "plane", [(p, p ^ bits) for p in range(N_PLANE)])

    band = exchange(columns(slab_cells, slab_weight, table))
    lines = rows(band, table, ell_index.T)
    across = swap(lines, 1)
    group = [lines, across]
    for part in (lines, across):
        group += [swap(part, bits) for bits in (2, 6, 4)]
    kappa, sums, ell, own = modes(kernel_index, kernel_table.reshape(1, -1), group, order)
    spectra, adjoint_band = adjoint(
        own, exchange(sums), kappa, ell, target_spectra, table
    )
    return spectra, maps(exchange(adjoint_band), table)


def solution(mesh):
    return jax.shard_map(
        body,
        mesh=mesh,
        in_specs=(
            P("plane", None, "tile", None),
            P("plane", None),
            P(),
            P(),
            P("plane", "tile"),
            P(),
        ),
        out_specs=(P(), P("plane", "tile", None)),
        check_vma=False,
    )
```

```python
import functools
import math

import jax
import jax.numpy as jnp
import ml_dtypes
import numpy as np
from jax import lax
from jax.experimental import pallas as pl
from jax.experimental.pallas import tpu as pltpu
from jax.sharding import PartitionSpec as P

NPIX = 4096
KMAX = 512
BINS = 4
ELLS = 16
RADIX = 8
SPAN = NPIX // RADIX
N_PLANE = 8
N_TILE = 32
ROWS = NPIX // N_TILE
LANES = 128
CHUNK = 16
WIDTH = 2 * KMAX + ROWS
PAIRS = BINS * (BINS + 1) // 2
CHUNKS = ROWS // CHUNK
STRIP = 32
STRIPS = ROWS // STRIP

ORDER = (0, 4, 1, 7, 2, 6, 3, 5)
PLACE = {rho: place for place, rho in enumerate(ORDER)}
DUOS = ((1, 7), (2, 6), (3, 5))
HALF = math.sqrt(0.5)

PAIR_ID = {}
for _number, (_i, _j) in enumerate(zip(*np.triu_indices(BINS))):
    PAIR_ID[(int(_i), int(_j))] = PAIR_ID[(int(_j), int(_i))] = _number
FIRST_GROUP = ((0, 0), (1, 1), (2, 2), (3, 3), (0, 1), (1, 2), (2, 3), (3, 0))
SECOND_GROUP = ((0, 2), (1, 3))

F32 = jnp.float32
BF16 = jnp.bfloat16
VMEM = pl.BlockSpec(memory_space=pltpu.VMEM)
SMEM = pl.BlockSpec(memory_space=pltpu.SMEM)
LIMIT = 32 * 1024 * 1024


def wave_table():
    rows = []
    tiles = np.arange(N_TILE)
    for rho in ORDER:
        k = np.concatenate([16 * tiles + 8 * kk + rho for kk in range(2)])
        m = (k[:, None] * np.arange(SPAN)[None, :]) % NPIX
        angle = 2.0 * np.pi * m / NPIX
        rows += [np.cos(angle), -np.sin(angle)]
    return np.concatenate(rows).astype(ml_dtypes.bfloat16)


def order_matrix():
    out = np.zeros((2 * KMAX, KMAX), np.float32)
    for place, rho in enumerate(ORDER):
        for kk in range(2):
            for t in range(N_TILE):
                j = 16 * t + 8 * kk + rho
                n = place * 64 + kk * N_TILE + t
                out[KMAX + j, n] = 1.0
                out[KMAX - j if j else 0, n] = 1.0
    return out.astype(ml_dtypes.bfloat16)


def edge_waves():
    step = lax.broadcasted_iota(jnp.int32, (1, SPAN), 1) & 7
    diag = jnp.where(step & 1 == 1, HALF, 1.0)
    cos = jnp.where(step & 3 == 2, 0.0, jnp.where((step >= 3) & (step <= 5), -diag, diag))
    sin = jnp.where(step & 3 == 0, 0.0, jnp.where(step >= 5, -diag, diag))
    return cos.astype(F32), sin.astype(F32)


def dft4(x, sign):
    (r0, i0), (r1, i1), (r2, i2), (r3, i3) = x
    ar, ai, br, bi = r0 + r2, i0 + i2, r0 - r2, i0 - i2
    cr, ci, dr, di = r1 + r3, i1 + i3, r1 - r3, i1 - i3
    if sign < 0:
        dr, di = -dr, -di
    return [(ar + cr, ai + ci), (br - di, bi + dr), (ar - cr, ai - ci), (br + di, bi - dr)]


def dft8(x, sign):
    even = dft4(x[0::2], sign)
    odd = dft4(x[1::2], sign)
    (r1, i1), (r2, i2), (r3, i3) = odd[1:]
    if sign > 0:
        turned = [odd[0], (HALF * (r1 - i1), HALF * (r1 + i1)), (-i2, r2), (-HALF * (r3 + i3), HALF * (r3 - i3))]
    else:
        turned = [odd[0], (HALF * (r1 + i1), HALF * (i1 - r1)), (i2, -r2), (HALF * (i3 - r3), -HALF * (r3 + i3))]
    low = [(a + c, b + d) for (a, b), (c, d) in zip(even, turned)]
    high = [(a - c, b - d) for (a, b), (c, d) in zip(even, turned)]
    return low + high


def dot_nt(a, b):
    return lax.dot_general(a, b, (((1,), (1,)), ((), ())), preferred_element_type=F32)


def dot_nn(a, b):
    return lax.dot_general(a, b, (((1,), (0,)), ((), ())), preferred_element_type=F32)


def dot_tn(a, b):
    return lax.dot_general(a, b, (((0,), (0,)), ((), ())), preferred_element_type=F32)


def table_of(table_ref, *rhos):
    start = PLACE[rhos[0]] * LANES
    return table_ref[start : start + LANES * len(rhos), :]


def columns_kernel(
    weight_ref, slab_ref, table_ref, out_ref, cells_ref, held_ref, fold_ref, band_ref,
    scale_ref, sems, table_sem, scale_sem,
):
    def fetch(chunk):
        rows = pl.ds(chunk * CHUNK, CHUNK)
        return pltpu.make_async_copy(slab_ref.at[0, :, rows, :], cells_ref.at[chunk], sems.at[chunk])

    def fetch_table():
        return pltpu.make_async_copy(table_ref, held_ref, table_sem)

    for chunk in range(8):
        fetch(chunk).start()
    scales = pltpu.make_async_copy(weight_ref, scale_ref, scale_sem)
    scales.start()
    fetch_table().start()
    scales.wait()
    weights = [scale_ref[0, layer] for layer in range(slab_ref.shape[1])]

    def butterfly(chunk, start):
        def segment(m):
            cols = slice(m * SPAN + start, m * SPAN + start + LANES)
            total = cells_ref[chunk, 0, :, cols].astype(F32) * weights[0]
            for layer in range(1, len(weights)):
                total = total + cells_ref[chunk, layer, :, cols].astype(F32) * weights[layer]
            return total

        def keep(index, value):
            fold_ref[index, chunk * CHUNK : (chunk + 1) * CHUNK, start : start + LANES] = value.astype(BF16)

        x0, x4 = segment(0), segment(4)
        a0, a1 = x0 + x4, x0 - x4
        x2, x6 = segment(2), segment(6)
        a2, a3 = x2 + x6, x2 - x6
        x1, x5 = segment(1), segment(5)
        b0, b1 = x1 + x5, x1 - x5
        x3, x7 = segment(3), segment(7)
        b2, b3 = x3 + x7, x3 - x7
        total, other = a0 + a2, b0 + b2
        keep(0, total + other)
        keep(1, total - other)
        minus, plus = HALF * (b1 - b3), HALF * (b1 + b3)
        keep(2, a1 + minus)
        keep(3, -a3 - plus)
        keep(4, a0 - a2)
        keep(5, b2 - b0)
        keep(6, a1 - minus)
        keep(7, a3 - plus)

    for chunk in range(CHUNKS):
        fetch(chunk).wait()
        if chunk + 8 < CHUNKS:
            fetch(chunk + 8).start()
        for start in range(0, SPAN, LANES):
            butterfly(chunk, start)
    fetch_table().wait()

    def place(rho, re, im):
        for s, part in enumerate((re, im)):
            for kk in range(2):
                start = 16 * s + 8 * kk + rho
                band_ref[pl.ds(start, N_TILE, stride=32), :] = part[kk * N_TILE : (kk + 1) * N_TILE]

    for rho in (0, 4):
        got = dot_nt(table_of(held_ref, rho), fold_ref[PLACE[rho]])
        place(rho, got[:64], got[64:])
    for number, (rho, back) in enumerate(DUOS):
        pair = fold_ref[2 + 2 * number : 4 + 2 * number].reshape(2 * ROWS, SPAN)
        got = dot_nt(table_of(held_ref, rho, back), pair)
        cu, cv = got[:64, :ROWS], got[:64, ROWS:]
        su, sv = got[64:128, :ROWS], got[64:128, ROWS:]
        place(rho, cu - sv, cv + su)
        cu, cv = got[128:192, :ROWS], got[128:192, ROWS:]
        su, sv = got[192:, :ROWS], got[192:, ROWS:]
        place(back, cu + sv, su - cv)
    out_ref[...] = band_ref[...].astype(BF16)


def columns(slab, weight, table):
    hbm = pl.BlockSpec(memory_space=pltpu.HBM)
    return pl.pallas_call(
        columns_kernel,
        in_specs=[hbm] * 3,
        out_specs=VMEM,
        out_shape=jax.ShapeDtypeStruct((2 * KMAX, ROWS), BF16),
        scratch_shapes=[
            pltpu.VMEM((CHUNKS, slab.shape[1], CHUNK, NPIX), BF16),
            pltpu.VMEM(table.shape, BF16),
            pltpu.VMEM((RADIX, ROWS, SPAN), BF16),
            pltpu.VMEM((2 * KMAX, ROWS), F32),
            pltpu.SMEM(weight.shape, F32),
            pltpu.SemaphoreType.DMA((CHUNKS,)),
            pltpu.SemaphoreType.DMA,
            pltpu.SemaphoreType.DMA,
        ],
        compiler_params=pltpu.CompilerParams(vmem_limit_bytes=53 * 1024 * 1024),
        name="columns",
    )(weight, slab, table)


def rows_kernel(band_ref, table_ref, ell_ref, out_ref, fold_ref):
    cos, sin = edge_waves()
    edge_re = jnp.zeros((16, 1), F32)
    edge_im = jnp.zeros((16, 1), F32)
    for u in range(SPAN // LANES):
        cols = slice(u * LANES, (u + 1) * LANES)
        starts = [(4 * m + u) * 32 for m in range(RADIX)]
        parts = [
            tuple(band_ref[start + 16 * s : start + 16 * s + 16, :].astype(F32) for s in range(2))
            for start in starts
        ]
        folded = dft8(parts, -1)
        for rho, (re, im) in enumerate(folded):
            fold_ref[PLACE[rho], 0:16, cols] = re.astype(BF16)
            fold_ref[PLACE[rho], 16:32, cols] = im.astype(BF16)
        up, vp = folded[0]
        edge_re = edge_re + jnp.sum(up * cos[:, cols] - vp * sin[:, cols], axis=1, keepdims=True)
        edge_im = edge_im + jnp.sum(vp * cos[:, cols] + up * sin[:, cols], axis=1, keepdims=True)
    lane = lax.broadcasted_iota(jnp.int32, (16, LANES), 1)
    low = lane < 64

    def lines(ahead, back):
        (cu, cv), (du, dv) = ahead, back
        real = jnp.where(low, cu - pltpu.roll(cv, 64, 1), pltpu.roll(du, 64, 1) + dv)
        imag = jnp.where(low, cv + pltpu.roll(cu, 64, 1), pltpu.roll(dv, 64, 1) - du)
        return real, imag

    def keep(rho, real, imag):
        cols = slice(PLACE[rho] * LANES, (PLACE[rho] + 1) * LANES)
        out_ref[0:16, cols] = real.astype(BF16)
        out_ref[16:32, cols] = imag.astype(BF16)

    for rho in (0, 4):
        got = dot_nt(fold_ref[PLACE[rho]], table_of(table_ref, rho))
        both = (got[:16], got[16:])
        real, imag = lines(both, both)
        if rho == 0:
            real = jnp.where(lane == 64, edge_re, real)
            imag = jnp.where(lane == 64, edge_im, imag)
        keep(rho, real, imag)
    for rho, back in DUOS:
        four = fold_ref[PLACE[rho] : PLACE[rho] + 2].reshape(64, SPAN)
        got = dot_nt(four, table_of(table_ref, rho, back))
        for place, one in enumerate((rho, back)):
            part = got[:, place * LANES : (place + 1) * LANES]
            duo = ((part[0:16], part[16:32]), (part[32:48], part[48:64]))
            keep(one, *lines(duo[place], duo[1 - place]))
    bins = ell_ref[...].astype(F32).astype(BF16)
    out_ref[0:16, 2 * KMAX :] = bins
    out_ref[16:32, 2 * KMAX :] = bins


def rows(band, table, ell):
    return pl.pallas_call(
        rows_kernel,
        in_specs=[VMEM, VMEM, VMEM],
        out_specs=VMEM,
        out_shape=jax.ShapeDtypeStruct((32, WIDTH), BF16),
        scratch_shapes=[pltpu.VMEM((RADIX, 32, SPAN), BF16)],
        compiler_params=pltpu.CompilerParams(vmem_limit_bytes=LIMIT),
        name="rows",
    )(band, table, ell)


def modes_kernel(
    index_ref, values_ref, *refs,
):
    (
        order_ref, kappa_ref, sums_ref, ell_ref, own_ref,
        lines_ref, terms_ref, picks_ref, entry_ref, value_ref,
    ) = refs[N_PLANE:]
    plane = lax.axis_index("plane")
    entry_ref[...] = jnp.zeros_like(entry_ref)
    entry_ref[0:BINS, 0:N_PLANE] = index_ref[...]
    value_ref[...] = jnp.zeros_like(value_ref)
    value_ref[:, 0 : values_ref.shape[1]] = jnp.broadcast_to(values_ref[...], (8, values_ref.shape[1]))
    kernel = jnp.take_along_axis(value_ref[...], entry_ref[...], axis=1)
    mine = jnp.where(lax.broadcasted_iota(jnp.int32, (8, LANES), 1) == plane, kernel, 0.0)
    own_ref[...] = jnp.broadcast_to(jnp.sum(mine, axis=1, keepdims=True), (8, LANES))
    for ref, bits in zip(refs, (0, 1, 2, 6, 4, 3, 7, 5)):
        lines_ref[plane ^ bits] = ref[...]
    bins = jnp.concatenate([lines_ref[p, 0:16, 2 * KMAX :] for p in range(N_PLANE)], axis=1)
    minus = dot_nn(bins[:, :KMAX], order_ref[:KMAX]).astype(jnp.int32)
    plus = dot_nn(bins[:, KMAX:], order_ref[KMAX:]).astype(jnp.int32)
    low = lax.broadcasted_iota(jnp.int32, (16, LANES), 1) < 64
    for pair in range(RADIX // 2):
        cols = slice(pair * LANES, (pair + 1) * LANES)
        ahead, back = plus[:, cols], minus[:, cols]
        ell_ref[:, 2 * pair * LANES : (2 * pair + 1) * LANES] = jnp.where(low, ahead, pltpu.roll(back, 64, 1))
        ell_ref[:, (2 * pair + 1) * LANES : (2 * pair + 2) * LANES] = jnp.where(low, pltpu.roll(ahead, 64, 1), back)
    weights = [
        [jnp.broadcast_to(kernel[b : b + 1, p : p + 1], (1, LANES)) for p in range(N_PLANE)] for b in range(BINS)
    ]
    for tile in range(RADIX):
        cols = slice(tile * LANES, (tile + 1) * LANES)
        kappa = [None] * BINS
        for p in range(N_PLANE):
            line = lines_ref[p, :, cols].astype(F32)
            for b in range(BINS):
                term = line * weights[b][p]
                kappa[b] = term if p == 0 else kappa[b] + term
        for b in range(BINS):
            kappa_ref[32 * b : 32 * b + 32, cols] = kappa[b]
        for number, (i, j) in enumerate(FIRST_GROUP + SECOND_GROUP):
            both = kappa[i] * kappa[j]
            term = both[0:16] + both[16:32]
            high = term.astype(BF16)
            terms_ref[16 * number : 16 * number + 16, cols] = high
            terms_ref[16 * (PAIRS + number) : 16 * (PAIRS + number) + 16, cols] = (
                term - high.astype(F32)
            ).astype(BF16)

    bin_row = lax.broadcasted_iota(jnp.int32, (16, 2 * KMAX), 0)
    for column in range(16):
        here = ell_ref[column : column + 1, :] == bin_row
        picks_ref[16 * column : 16 * column + 16, :] = jnp.where(here, 1.0, 0.0).astype(BF16)
    crossed = dot_nt(terms_ref[...], picks_ref[...])
    same = (lax.broadcasted_iota(jnp.int32, (16, 2 * LANES), 1) >> 4) == lax.broadcasted_iota(
        jnp.int32, (16, 2 * LANES), 0
    )
    lane = lax.broadcasted_iota(jnp.int32, (8, LANES), 1)
    sub = lax.broadcasted_iota(jnp.int32, (8, LANES), 0)
    spread = [jnp.zeros((8, LANES), F32), jnp.zeros((8, LANES), F32)]
    for number in range(PAIRS):
        low = 16 * (PAIRS + number)
        part = crossed[16 * number : 16 * number + 16] + crossed[low : low + 16]
        part = jnp.where(same, part, 0.0)
        part = part[0:8] + part[8:16]
        total = jnp.sum(part[:, :LANES] + part[:, LANES:], axis=0, keepdims=True)
        for shift in (64, 32, 16):
            total = total + pltpu.roll(total, shift, 1)
        group, row = divmod(number, 8)
        spread[group] = jnp.where(sub == row, total, spread[group])
    own = (lane >> 4) == sub
    sums = [jnp.sum(jnp.where(own, part, 0.0), axis=0, keepdims=True) for part in spread]
    pattern = jnp.where(sub & 1 == 0, sums[0], sums[1])
    sums_ref[...] = jnp.broadcast_to(pattern[None], (N_TILE // 4, 8, LANES)).reshape(2 * N_TILE, LANES)


def modes(index, values, group, order):
    return pl.pallas_call(
        modes_kernel,
        in_specs=[VMEM] * 11,
        out_specs=[VMEM] * 4,
        out_shape=[
            jax.ShapeDtypeStruct((32 * BINS, 2 * KMAX), F32),
            jax.ShapeDtypeStruct((2 * N_TILE, LANES), F32),
            jax.ShapeDtypeStruct((16, 2 * KMAX), jnp.int32),
            jax.ShapeDtypeStruct((8, LANES), F32),
        ],
        scratch_shapes=[
            pltpu.VMEM((N_PLANE, 32, WIDTH), BF16),
            pltpu.VMEM((2 * PAIRS * 16, 2 * KMAX), BF16),
            pltpu.VMEM((16 * ELLS, 2 * KMAX), BF16),
            pltpu.VMEM((8, LANES), jnp.int32),
            pltpu.VMEM((8, LANES), F32),
        ],
        compiler_params=pltpu.CompilerParams(vmem_limit_bytes=LIMIT),
        name="modes",
    )(index, values, *group, order)


def adjoint_kernel(
    own_ref, sums_ref, kappa_ref, ell_ref, target_ref, table_ref,
    spectra_ref, out_ref, weight_ref, line_ref, spread_ref,
):
    total = jnp.sum(sums_ref[...].reshape(N_TILE // 4, 8, LANES), axis=0)
    total = total + pltpu.roll(total, 2, 0)
    total = total + pltpu.roll(total, 4, 0)
    lane = lax.broadcasted_iota(jnp.int32, (1, LANES), 1)
    area = (2.0 * lane.astype(F32) + 1.0) * (float((KMAX // ELLS) ** 2) * (0.5 * math.pi))
    scale = float(NPIX * NPIX) * area
    for row, group in enumerate((FIRST_GROUP, SECOND_GROUP)):
        line = total[row : row + 1, :]
        for place, pair in enumerate(group):
            turned = line if place == 0 else pltpu.roll(line, LANES - 16 * place, 1)
            number = PAIR_ID[pair]
            spectra_ref[number : number + 1, :] = (turned / scale)[:, :ELLS]
    weight_ref[...] = jnp.zeros_like(weight_ref)
    weight_ref[0:10, 0:ELLS] = (spectra_ref[...] - target_ref[...]) * (
        float(KMAX) / (ELLS * NPIX)
    ) / area[:, :ELLS]

    tables = []
    for j in range(BINS):
        total = None
        for i in range(BINS):
            number = PAIR_ID[(i, j)]
            row = weight_ref[number : number + 1, :]
            term = own_ref[i : i + 1, :] * (row + row if i == j else row)
            total = term if total is None else total + term
        tables.append(jnp.broadcast_to(total, (8, LANES)))

    for tile in range(RADIX):
        cols = slice(tile * LANES, (tile + 1) * LANES)
        for half in range(0, 16, 8):
            where = ell_ref[half : half + 8, cols]
            mixers = [jnp.take_along_axis(table, where, axis=1) for table in tables]
            for s in range(2):
                start = 16 * s + half
                line = mixers[0] * kappa_ref[start : start + 8, cols]
                for j in range(1, BINS):
                    line = line + mixers[j] * kappa_ref[32 * j + start : 32 * j + start + 8, cols]
                line_ref[start : start + 8, cols] = line

    wide_lane = lax.broadcasted_iota(jnp.int32, (16, LANES), 1)
    low = wide_lane < 64

    def factors(rho):
        cols = slice(PLACE[rho] * LANES, (PLACE[rho] + 1) * LANES)
        g0, g1 = line_ref[0:16, cols], line_ref[16:32, cols]
        if rho == 0:
            g0 = jnp.where(wide_lane == 64, 0.0, g0)
            g1 = jnp.where(wide_lane == 64, 0.0, g1)
        t0, t1 = pltpu.roll(g0, 64, 1), pltpu.roll(g1, 64, 1)
        ahead = (jnp.where(low, g0, t1), jnp.where(low, g1, -t0))
        back = (jnp.where(low, t0, -g1), jnp.where(low, t1, g0))
        return ahead, back

    def spread(rho, re, im):
        spread_ref[2 * rho] = re
        spread_ref[2 * rho + 1] = im

    start = PLACE[0] * LANES + 64
    edge0 = line_ref[0:16, start : start + 1]
    edge1 = line_ref[16:32, start : start + 1]
    cos, sin = edge_waves()
    for rho in (0, 4):
        ahead, back = factors(rho)
        left = jnp.concatenate([ahead[0] + back[0], ahead[1] + back[1]], axis=0).astype(BF16)
        got = dot_nn(left, table_of(table_ref, rho))
        re, im = got[:16], got[16:]
        if rho == 0:
            re = re + edge0 * cos + edge1 * sin
            im = im + edge1 * cos - edge0 * sin
        spread(rho, re, im)
    for rho, back in DUOS:
        plus, minus = factors(rho)
        plus_back, minus_back = factors(back)
        left = jnp.concatenate(
            [
                jnp.concatenate(plus + minus, axis=0),
                jnp.concatenate(minus_back + plus_back, axis=0),
            ],
            axis=1,
        ).astype(BF16)
        got = dot_nn(left, table_of(table_ref, rho, back))
        spread(rho, got[0:16], got[16:32])
        spread(back, got[32:48], got[48:64])
    for u in range(SPAN // LANES):
        cols = slice(u * LANES, (u + 1) * LANES)
        parts = [(spread_ref[2 * rho, :, cols], spread_ref[2 * rho + 1, :, cols]) for rho in range(RADIX)]
        for m, both in enumerate(dft8(parts, 1)):
            for s in range(2):
                begin = (4 * m + u) * 32 + 16 * s
                out_ref[begin : begin + 16, :] = both[s].astype(BF16)


def adjoint(own, sums, kappa, ell, target, table):
    return pl.pallas_call(
        adjoint_kernel,
        in_specs=[VMEM] * 6,
        out_specs=[VMEM, VMEM],
        out_shape=[
            jax.ShapeDtypeStruct(target.shape, F32),
            jax.ShapeDtypeStruct((2 * KMAX, ROWS), BF16),
        ],
        scratch_shapes=[
            pltpu.VMEM((16, LANES), F32),
            pltpu.VMEM((32, 2 * KMAX), F32),
            pltpu.VMEM((2 * RADIX, 16, SPAN), F32),
        ],
        compiler_params=pltpu.CompilerParams(vmem_limit_bytes=LIMIT),
        name="adjoint",
    )(own, sums, kappa, ell, target, table)


def maps_kernel(band_ref, table_ref, out_ref, wide_ref, spread_ref, done_ref, sems):
    wide_ref[...] = band_ref[...].astype(F32)

    def block(rho, s):
        parts = [
            wide_ref[pl.ds(16 * s + 8 * kk + rho, N_TILE, stride=32), :] for kk in range(2)
        ]
        return jnp.concatenate(parts, axis=0)

    flat = []
    for rho in (0, 4):
        left = jnp.concatenate([block(rho, 0), block(rho, 1)], axis=0).astype(BF16)
        flat.append(dot_tn(left, table_of(table_ref, rho)))
    p, q = [None], [None]
    for rho, back in DUOS:
        b0, b1, e0, e1 = block(rho, 0), block(rho, 1), block(back, 0), block(back, 1)
        left = jnp.concatenate(
            [
                jnp.concatenate([b0, b1, e0, e1], axis=0),
                jnp.concatenate([b1, -b0, -e1, e0], axis=0),
            ],
            axis=1,
        ).astype(BF16)
        got = dot_tn(left, table_of(table_ref, rho, back))
        p.append(got[:ROWS])
        q.append(got[ROWS:])
    for index, part in enumerate(flat + p[1:] + q[1:]):
        spread_ref[index] = part

    def send(chunk):
        rows = pl.ds(chunk * STRIP, STRIP)
        return pltpu.make_async_copy(done_ref.at[rows, :], out_ref.at[0, rows, :], sems.at[chunk])

    for chunk in range(STRIPS):
        rows = slice(chunk * STRIP, (chunk + 1) * STRIP)
        for start in range(0, SPAN, LANES):
            cols = slice(start, start + LANES)
            a0, a4, p1, p2, p3, q1, q2, q3 = (spread_ref[index, rows, cols] for index in range(RADIX))

            def put(m, even, odd):
                done_ref[rows, m * SPAN + start : m * SPAN + start + LANES] = even + odd
                done_ref[rows, (m + 4) * SPAN + start : (m + 4) * SPAN + start + LANES] = even - odd

            plus, minus = a0 + a4, a0 - a4
            put(0, plus + p2, p1 + p3)
            put(1, minus - q2, HALF * (p1 - q1 - p3 - q3))
            put(2, plus - p2, q3 - q1)
            put(3, minus + q2, HALF * (p3 - p1 - q1 - q3))
        send(chunk).start()
    for chunk in range(STRIPS):
        send(chunk).wait()


def maps(band, table):
    return pl.pallas_call(
        maps_kernel,
        in_specs=[VMEM, VMEM],
        out_specs=pl.BlockSpec(memory_space=pltpu.HBM),
        out_shape=jax.ShapeDtypeStruct((1, ROWS, NPIX), F32),
        scratch_shapes=[
            pltpu.VMEM((2 * KMAX, ROWS), F32),
            pltpu.VMEM((RADIX, ROWS, SPAN), F32),
            pltpu.VMEM((ROWS, NPIX), F32),
            pltpu.SemaphoreType.DMA((STRIPS,)),
        ],
        compiler_params=pltpu.CompilerParams(vmem_limit_bytes=LIMIT),
        name="maps",
    )(band, table)


def body(slab_cells, slab_weight, kernel_table, kernel_index, ell_index, target_spectra):
    table = jnp.asarray(wave_table())
    order = jnp.asarray(order_matrix())
    exchange = functools.partial(
        lax.all_to_all, axis_name="tile", split_axis=0, concat_axis=0, tiled=True
    )

    def swap(value, bits):
        return lax.ppermute(value, "plane", [(p, p ^ bits) for p in range(N_PLANE)])

    band = exchange(columns(slab_cells, slab_weight, table))
    lines = rows(band, table, ell_index.T)
    across = swap(lines, 1)
    group = [lines, across]
    for part in (lines, across):
        group += [swap(part, bits) for bits in (2, 6, 4)]
    kappa, sums, ell, own = modes(kernel_index, kernel_table.reshape(1, -1), group, order)
    spectra, adjoint_band = adjoint(
        own, exchange(sums), kappa, ell, target_spectra, table
    )
    return spectra, maps(exchange(adjoint_band), table)


def solution(mesh):
    return jax.shard_map(
        body,
        mesh=mesh,
        in_specs=(
            P("plane", None, "tile", None),
            P("plane", None),
            P(),
            P(),
            P("plane", "tile"),
            P(),
        ),
        out_specs=(P(), P("plane", "tile", None)),
        check_vma=False,
    )
```
